256 devices in a mesh: seq: 32 (over z, x), head: 8 (over y, core).
Axes of the slice: x: 4, y: 4, z: 8, core: 2. Of those that a mesh axis runs over, the one named last changes fastest.
Arguments:
- queries: bfloat16 [32768, 2048], P('seq', 'head'), may hold values from -108 to 108
- pool: bfloat16 [1024, 128, 896], P('seq', 'head'), may hold values from -6 to 6
- w_key: bfloat16 [896, 2048], P(None, 'head'), may hold values from -0.1875 to 0.1875
- w_value: bfloat16 [896, 2048], P(None, 'head'), may hold values from -0.1875 to 0.1875
- out_grad: bfloat16 [32768, 2048], P('seq', 'head'), may hold values from -1.5 to 1.5
- nb_source: int32 [512, 2], replicated, may hold values from 0 to 31, all different within a row; in each aligned block of 16 rows (0 to 15, 16 to 31, ...) at most 2 rows name the same one
- nb_slot: int32 [512, 2], replicated, may hold values from 0 to 31
- nb_count: int32 [512], replicated, may hold values from 1 to 2
Outputs:
- attended: bfloat16 [32768, 2048], P('seq', 'head')
- grad_queries: bfloat16 [32768, 2048], P('seq', 'head')
- grad_pool: float32 [1024, 128, 896], P('seq', 'head')
- grad_w_key: float32 [896, 2048], P(None, 'head')
- grad_w_value: float32 [896, 2048], P(None, 'head')
The draws below stay inside these ranges and needn't reach their ends.
Inputs may be any that keep to these rules, and one draw needn't show every extreme that they name: `nb_source`: for the 16 stretches of one device (aligned blocks of stretches), no encoder device is named by more than 2 entries, and in some block one is named exactly 2 times; the 2 neighbours of a stretch come from different encoder devices.
All inputs are finite; a program needn't handle non-finite values.
Results may differ from the reference program's by a relative error of at most 0.018.
The reference program's roundings to bfloat16 on the way count: a program that leaves them out, or rounds other values in their place, can miss the bound.
Values may be sent and summed in bfloat16 or wider, within the bound.
No kernel may reach another device: no remote copies, remote signals or barrier semaphores. Data moves between devices by JAX's collectives and lax.ppermute only.
A program may use at most 128 MiB of HBM per device.

```python
import math
import jax
import jax.numpy as jnp
import numpy as np
from jax import lax

HEADS = 16
DH = 128
E = 896
STRETCH = 64
R = 128
KNB = 2
CH_DEV = 16
POOL = 32
CAP = 2
D = 2048
TOKENS = 32768
STRETCHES = 512
POOL_ALL = 1024
N_SEQ = 32
N_HEAD = 8


def draw_queries(key, part):
    base = jax.random.truncated_normal(key, -6.0, 6.0, (TOKENS, D), jnp.float32)
    return base.astype(jnp.bfloat16)


def with_ends(array, key, low, high):
    extent = array.shape
    index_at = [jax.random.randint(jax.random.fold_in(key, axis), (), 0, extent[axis]) for axis in range(len(extent))]
    array = array.at[tuple(index_at)].set(low)
    longest = extent.index(max(extent))
    index_at[longest] = (index_at[longest] + 1) % extent[longest]
    return array.at[tuple(index_at)].set(high)


def block_levels(key, dims, split, low, high):
    gain = 1.0
    for dim, blocks in split:
        steps = jax.random.uniform(jax.random.fold_in(jax.random.fold_in(key, 6), dim), (blocks,), jnp.float32, low / len(split), high / len(split))
        gain = gain * jnp.repeat(jnp.exp(steps), dims[dim] // blocks).reshape((-1,) + (1,) * (len(dims) - 1 - dim))
    return gain


def shared_out(key, own, number, rows, amount, top, bound, slope):
    sequence = jax.random.permutation(key, amount)
    crowded, ordinary = load_shares(amount, rows * top, bound, slope, True), load_shares(amount, rows * top, bound, slope, False)
    places = jnp.arange(amount)

    def named(sizes, turn):
        used = int((sizes > 0).sum())
        fixed = max(1, used // 4)
        passed = fixed + (places - fixed + turn * (used - fixed)) % max(1, amount - fixed)
        return jnp.zeros((amount,), jnp.int32).at[sequence[jnp.where(places < fixed, places, passed)]].set(jnp.asarray(sizes, jnp.int32))

    sizes = jnp.where(number % 4 == 0, named(crowded, number // 4), named(ordinary, number - number // 4 - 1))
    mixed = jax.random.permutation(jax.random.fold_in(own, 3), amount)
    donor, taker = mixed[0:amount // 2 * 2:2], mixed[1:amount // 2 * 2:2]
    margin = jnp.minimum(sizes[donor] - 1, bound - sizes[taker]) // 2
    margin = jnp.where((donor == sequence[0]) | (taker == sequence[0]) | (sizes[taker] == 0), 0, jnp.maximum(margin, 0))
    passed = jax.random.randint(jax.random.fold_in(own, 4), (amount // 2,), 0, 1 << 20) % (margin + 1)
    sizes = sizes.at[donor].add(-passed).at[taker].add(passed)
    labels = jnp.searchsorted(jnp.cumsum(sizes), jnp.arange(rows * top), side="right").astype(jnp.int32)
    table = labels.reshape(top, rows).T
    table = table[jax.random.permutation(jax.random.fold_in(own, 1), rows)]
    turn = jax.random.randint(jax.random.fold_in(own, 2), (rows, 1), 0, top)
    return jnp.take_along_axis(table, (jnp.arange(top)[None, :] + turn) % top, axis=1)


def load_shares(count, total, bound, skew, full):
    weights = [(1 << 20) // math.isqrt(standing ** skew) + 1 for standing in range(1, count + 1)]
    largest = bound if full else min(bound, max(-(-total // count), total * weights[0] // sum(weights)))
    least = 1 if total - largest >= count - 1 else 0
    holding, rest = [largest] + [least] * (count - 1), total - largest - least * (count - 1)
    while rest > 0:
        movable = [i for i in range(1, count) if holding[i] < largest] or [i for i in range(1, count) if holding[i] < bound]
        whole, left = sum([weights[i] for i in movable]), rest
        for i in movable:
            more = min(bound - holding[i], max(1, left * weights[i] // whole), rest)
            holding[i] = holding[i] + more
            rest = rest - more
    return np.array(holding)


def normal_values(key, extent, spread, most, shards=(), kind=jnp.bfloat16):
    factor_of = block_levels(key, extent, shards, -0.22, 0.18) if shards else 1.0
    drawn = jax.random.normal(key, extent, jnp.float32) * spread * factor_of
    return jnp.minimum(jnp.maximum(drawn, -most), most).astype(kind)


def setup_inputs(seed: int = 0) -> dict:
    key_of = jax.random.split(jax.random.key(seed), 9)
    queries = draw_queries(jax.random.fold_in(key_of[8], 71), 0)
    pool = normal_values(key_of[1], (POOL_ALL, R, E), 1.0, 6.0, ((0, 32), (1, 8)))
    w_key = normal_values(key_of[2], (E, D), E ** -0.5, 0.1875, ((1, 8),))
    w_value = normal_values(key_of[3], (E, D), E ** -0.5, 0.1875, ((1, 8),))
    out_grad = normal_values(key_of[4], (TOKENS, D), 0.25, 1.5, ((0, 32), (1, 8)))
    nb_source_keys = jax.random.split(jax.random.fold_in(key_of[5], 1), STRETCHES // CH_DEV)
    nb_source_turns = jax.random.permutation(jax.random.fold_in(key_of[5], 3), STRETCHES // CH_DEV)
    nb_source = jax.vmap(lambda own, number: shared_out(jax.random.fold_in(key_of[5], 2), own, number, CH_DEV, N_SEQ, KNB, CAP, 2))(nb_source_keys, nb_source_turns).reshape((STRETCHES, KNB))
    nb_slot = with_ends(jax.random.randint(key_of[6], (STRETCHES, KNB), 0, POOL), jax.random.fold_in(key_of[6], 1), 0, POOL - 1).astype(jnp.int32)
    nb_count = with_ends(jax.random.randint(key_of[7], (STRETCHES,), 1, KNB + 1), jax.random.fold_in(key_of[7], 1), 1, KNB).astype(jnp.int32)
    return dict(queries=queries, pool=pool, w_key=w_key, w_value=w_value, out_grad=out_grad, nb_source=nb_source, nb_slot=nb_slot, nb_count=nb_count)


def reference(queries, pool, w_key, w_value, out_grad, nb_source, nb_slot, nb_count):
    f32 = jnp.float32
    requests = CH_DEV * KNB
    factor = 1.0 / math.sqrt(DH)
    index_table = (nb_source * POOL + nb_slot).astype(jnp.int32).reshape(N_SEQ, requests)
    query_all = queries.reshape(N_SEQ, CH_DEV, STRETCH, HEADS, DH)
    grad_all = out_grad.reshape(N_SEQ, CH_DEV, STRETCH, HEADS, DH)
    count_all = nb_count.reshape(N_SEQ, CH_DEV)
    both_weights = jnp.concatenate([w_key, w_value], axis=1).astype(f32)
    group_width = D // N_HEAD
    key_groups = w_key.astype(f32).reshape(E, N_HEAD, group_width)
    value_groups = w_value.astype(f32).reshape(E, N_HEAD, group_width)

    def per_owner(carry, inputs):
        grad_wk, grad_wv = carry
        index_row, query_blocks, grad_blocks, used_counts = inputs
        panels = pool[index_row]
        joined = jnp.einsum('jre,ec->jrc', panels.astype(f32), both_weights).astype(jnp.bfloat16)
        keys = joined[:, :, :D].reshape(CH_DEV, KNB, R, HEADS, DH)
        values = joined[:, :, D:].reshape(CH_DEV, KNB, R, HEADS, DH)
        query_f = query_blocks.astype(f32)
        grad_f = grad_blocks.astype(f32)
        keys_f = keys.astype(f32)
        values_f = values.astype(f32)
        scores = jnp.einsum('cqhd,ckrhd->chqkr', query_f, keys_f) * factor
        used_mask = (jnp.arange(KNB)[None, :] < used_counts[:, None])[:, None, None, :, None]
        masked_scores = jnp.where(used_mask, scores, -jnp.inf)
        row_max = lax.optimization_barrier(jnp.max(masked_scores, axis=(3, 4), keepdims=True))
        exp_scores = jnp.where(used_mask, jnp.exp(masked_scores - row_max), 0.0)
        soft_probs = exp_scores / lax.optimization_barrier(jnp.sum(exp_scores, axis=(3, 4), keepdims=True))
        soft_weights = soft_probs.astype(jnp.bfloat16)
        weights_f = soft_weights.astype(f32)
        attended = jnp.einsum('chqkr,ckrhd->cqhd', weights_f, values_f).astype(jnp.bfloat16)
        grad_probs = jnp.einsum('cqhd,ckrhd->chqkr', grad_f, values_f)
        row_dot = lax.optimization_barrier(jnp.sum(soft_probs * grad_probs, axis=(3, 4), keepdims=True))
        grad_scores = (soft_probs * (grad_probs - row_dot)).astype(jnp.bfloat16).astype(f32)
        grad_queries = (jnp.einsum('chqkr,ckrhd->cqhd', grad_scores, keys_f) * factor).astype(jnp.bfloat16)
        grad_keys = (jnp.einsum('chqkr,cqhd->ckrhd', grad_scores, query_f) * factor).astype(jnp.bfloat16)
        grad_values = jnp.einsum('chqkr,cqhd->ckrhd', weights_f, grad_f).astype(jnp.bfloat16)
        grad_keys = grad_keys.reshape(requests, R, N_HEAD, group_width).astype(f32)
        grad_values = grad_values.reshape(requests, R, N_HEAD, group_width).astype(f32)
        partial_sum = jnp.einsum('jrgc,egc->gjre', grad_keys, key_groups) + jnp.einsum('jrgc,egc->gjre', grad_values, value_groups)
        shares = lax.optimization_barrier(partial_sum.astype(jnp.bfloat16))
        contribution = lax.optimization_barrier(jnp.sum(shares.astype(f32), axis=0)).astype(jnp.bfloat16)
        panels_f = panels.astype(f32)
        grad_wk = grad_wk + jnp.einsum('jre,jrc->ec', panels_f, grad_keys.reshape(requests, R, D))
        grad_wv = grad_wv + jnp.einsum('jre,jrc->ec', panels_f, grad_values.reshape(requests, R, D))
        return ((grad_wk, grad_wv), (attended, grad_queries, contribution))
    start_carry = (jnp.zeros((E, D), f32), jnp.zeros((E, D), f32))
    (grad_w_key, grad_w_value), (attended, grad_queries, contributions) = lax.scan(per_owner, start_carry, (index_table, query_all, grad_all, count_all))
    flat_index = index_table.reshape(N_SEQ * requests)
    grad_pool = jnp.zeros((N_SEQ * POOL, R, E), f32).at[flat_index].add(contributions.reshape(N_SEQ * requests, R, E).astype(f32))
    return (attended.reshape(TOKENS, D), grad_queries.reshape(TOKENS, D), grad_pool, grad_w_key, grad_w_value)
```

```python
import math

import jax
import jax.numpy as jnp
from jax import lax
from jax.experimental import pallas as pl
from jax.experimental.pallas import tpu as pltpu
from jax.sharding import Mesh
from jax.sharding import PartitionSpec as P

DH = 128
STRETCH = 64
KNB = 2
CH_DEV = 16
ROWS = 16
PIECES = 8
SPLIT = 512
GROUP = 2
F32 = jnp.float32
BF16 = jnp.bfloat16

UP = [(i, (i + 1) % 4) for i in range(4)]
DOWN = [((i + 1) % 4, i) for i in range(4)]
SWAP = [(0, 1), (1, 0)]


def dot(a, b, ca, cb):
    return lax.dot_general(a, b, (((ca,), (cb,)), ((), ())), preferred_element_type=F32)


def shift(size, k):
    return [(i, (i + k) % size) for i in range(size)]


def gather_pieces(own):
    half = own.shape[0] // 2
    below = lax.ppermute(own, "y", UP)
    above = lax.ppermute(own, "y", DOWN)
    far_low = lax.ppermute(below[:half], "y", UP)
    far_high = lax.ppermute(above[half:], "y", DOWN)
    mine = [own, above, below, far_low, far_high]
    return mine + [lax.ppermute(piece, "core", SWAP) for piece in mine]


def plus(*terms):
    total = terms[0].astype(F32)
    for term in terms[1:]:
        total = total + term.astype(F32)
    return total


def scatter_pieces(mine, other):
    swapped = lax.ppermute(other, "core", SWAP)
    half = mine.shape[1] // 2
    far = plus(mine[3], swapped[3]).astype(BF16)
    got_low = lax.ppermute(far[:half], "y", UP)
    got_high = lax.ppermute(far[half:], "y", DOWN)
    up_low = plus(mine[1, :half], swapped[1, :half], got_low).astype(BF16)
    up_high = plus(mine[1, half:], swapped[1, half:]).astype(BF16)
    down_low = plus(mine[2, :half], swapped[2, :half]).astype(BF16)
    down_high = plus(mine[2, half:], swapped[2, half:], got_high).astype(BF16)
    from_below = lax.ppermute(jnp.concatenate([up_low, up_high]), "y", UP)
    from_above = lax.ppermute(jnp.concatenate([down_low, down_high]), "y", DOWN)
    return plus(mine[0], swapped[0], from_below, from_above).astype(BF16)


def fill_rows(step, refs, rows_ref, lo, hi):
    half_steps = CH_DEV // GROUP // 2
    for core in range(2):
        own, above, below, far_low, far_high = refs[core * 5 : core * 5 + 5]

        def put(place, ref):
            for c in range(GROUP):
                at = c * KNB * ROWS * PIECES + (core * 4 + place) * KNB * ROWS
                rows_ref[at : at + KNB * ROWS, lo:hi] = ref[c * KNB : (c + 1) * KNB].reshape(
                    KNB * ROWS, hi - lo
                )

        put(0, own)
        put(1, above)
        put(2, below)

        @pl.when(step < half_steps)
        def _():
            put(3, far_low)

        @pl.when(step >= half_steps)
        def _():
            put(3, far_high)


def put_share(share, c, mine_ref, other_ref):
    width = share.shape[1]
    for piece in range(PIECES):
        ref = mine_ref if piece < 4 else other_ref
        at = piece * KNB * ROWS
        ref[piece % 4, c * KNB : (c + 1) * KNB] = share[at : at + KNB * ROWS].reshape(
            KNB, ROWS, width
        )


def attention_kernel(count_ref, *refs):
    pieces_a, pieces_b = refs[:10], refs[10:20]
    weight_ref, turned_ref, query_ref, grad_ref = refs[20:24]
    attended_ref, grad_query_ref, mine_ref, other_ref, both_ref = refs[24:29]
    rows_ref, kv_ref = refs[29:]
    step = pl.program_id(0)
    width = rows_ref.shape[1]
    fill_rows(step, pieces_a, rows_ref, 0, SPLIT)
    fill_rows(step, pieces_b, rows_ref, SPLIT, width)
    span = KNB * ROWS * PIECES
    factor = 1.0 / math.sqrt(DH)
    neighbour = (lax.broadcasted_iota(jnp.int32, (STRETCH, span), 1) // ROWS) % KNB
    kv_ref[...] = dot(rows_ref[...], weight_ref[...], 1, 0).astype(BF16)
    for c in range(GROUP):
        used = neighbour < count_ref[step * GROUP + c]
        rows = slice(c * span, (c + 1) * span)
        tokens = slice(c * STRETCH, (c + 1) * STRETCH)
        for h in range(2):
            cols = slice(h * DH, (h + 1) * DH)
            vcols = slice((2 + h) * DH, (3 + h) * DH)
            query, grad = query_ref[tokens, cols], grad_ref[tokens, cols]
            keys, values = kv_ref[rows, cols], kv_ref[rows, vcols]
            scores = jnp.where(used, dot(query, keys, 1, 1) * factor, -jnp.inf)
            top = jnp.max(scores, axis=1, keepdims=True)
            powers = jnp.exp(scores - top)
            probs = powers / jnp.sum(powers, axis=1, keepdims=True)
            weights = probs.astype(BF16)
            attended_ref[tokens, cols] = dot(weights, values, 1, 0).astype(BF16)
            dprobs = dot(grad, values, 1, 1)
            row_dot = jnp.sum(probs * dprobs, axis=1, keepdims=True)
            dscores = (probs * (dprobs - row_dot)).astype(BF16)
            grad_query_ref[tokens, cols] = (dot(dscores, keys, 1, 0) * factor).astype(BF16)
            both_ref[rows, cols] = (dot(dscores, query, 0, 0) * factor).astype(BF16)
            both_ref[rows, vcols] = dot(weights, grad, 0, 0).astype(BF16)
    for c in range(GROUP):
        share = dot(both_ref[c * span : (c + 1) * span, :], turned_ref[...], 1, 0).astype(BF16)
        put_share(share, c, mine_ref, other_ref)


def weight_kernel(*refs):
    pieces_a, pieces_b = refs[:10], refs[10:20]
    turned_ref, both_ref = refs[20:22]
    mine_ref, other_ref, out_ref = refs[22:25]
    rows_ref, total_ref = refs[25:]
    step = pl.program_id(0)
    width = rows_ref.shape[1]
    span = KNB * ROWS * PIECES
    fill_rows(step, pieces_a, rows_ref, 0, SPLIT)
    fill_rows(step, pieces_b, rows_ref, SPLIT, width)
    for c in range(GROUP):
        share = dot(both_ref[c * span : (c + 1) * span, :], turned_ref[...], 1, 0).astype(BF16)
        put_share(share, c, mine_ref, other_ref)
    part = dot(rows_ref[...], both_ref[...], 0, 0)

    @pl.when(step == 0)
    def _():
        total_ref[...] = part

    @pl.when(step > 0)
    def _():
        total_ref[...] += part

    @pl.when(step == pl.num_programs(0) - 1)
    def _():
        for g in range(4):
            out_ref[g] = total_ref[:, g * DH : (g + 1) * DH].astype(BF16)


def piece_specs(width):
    half_steps = CH_DEV // GROUP // 2
    block = (GROUP * KNB, ROWS, width)
    plain = pl.BlockSpec(block, lambda i, *_: (i, 0, 0))
    low = pl.BlockSpec(block, lambda i, *_: (jnp.minimum(i, half_steps - 1), 0, 0))
    high = pl.BlockSpec(block, lambda i, *_: (jnp.maximum(i - half_steps, 0), 0, 0))
    return [plain, plain, plain, low, high] * 2


def share_out(width):
    spec = pl.BlockSpec((4, GROUP * KNB, ROWS, width), lambda i, *_: (0, i, 0, 0))
    shape = jax.ShapeDtypeStruct((4, CH_DEV * KNB, ROWS, width), BF16)
    return [spec, spec], [shape, shape]


def attention(counts, pieces_a, pieces_b, weight, turned_a, queries, out_grad):
    width = weight.shape[0]
    tokens, local = queries.shape
    span = GROUP * KNB * ROWS * PIECES
    steps = CH_DEV // GROUP
    token_spec = pl.BlockSpec((GROUP * STRETCH, local), lambda i, *_: (i, 0))
    whole = lambda a: pl.BlockSpec(a.shape, lambda i, *_: (0, 0))
    share_specs, share_shapes = share_out(SPLIT)
    return pl.pallas_call(
        attention_kernel,
        grid_spec=pltpu.PrefetchScalarGridSpec(
            num_scalar_prefetch=1,
            grid=(steps,),
            in_specs=piece_specs(SPLIT)
            + piece_specs(width - SPLIT)
            + [whole(weight), whole(turned_a), token_spec, token_spec],
            out_specs=[token_spec, token_spec]
            + share_specs
            + [pl.BlockSpec((span, 2 * local), lambda i, *_: (i, 0))],
            scratch_shapes=[pltpu.VMEM((span, width), BF16), pltpu.VMEM((span, 2 * local), BF16)],
        ),
        out_shape=[
            jax.ShapeDtypeStruct((tokens, local), BF16),
            jax.ShapeDtypeStruct((tokens, local), BF16),
        ]
        + share_shapes
        + [jax.ShapeDtypeStruct((span * steps, 2 * local), BF16)],
        compiler_params=pltpu.CompilerParams(vmem_limit_bytes=32 * 2**20),
        cost_estimate=pl.CostEstimate(
            flops=10 * 2**30, bytes_accessed=20 * 2**20, transcendentals=2**19
        ),
        name="attention",
    )(counts, *pieces_a, *pieces_b, weight, turned_a, queries, out_grad)


def weight_grads(pieces_a, pieces_b, turned_b, both, width):
    span = GROUP * KNB * ROWS * PIECES
    steps = CH_DEV // GROUP
    cols = both.shape[1]
    share_specs, share_shapes = share_out(width - SPLIT)
    return pl.pallas_call(
        weight_kernel,
        grid=(steps,),
        in_specs=piece_specs(SPLIT)
        + piece_specs(width - SPLIT)
        + [
            pl.BlockSpec(turned_b.shape, lambda i: (0, 0)),
            pl.BlockSpec((span, cols), lambda i: (i, 0)),
        ],
        out_specs=share_specs + [pl.BlockSpec((4, width, DH), lambda i: (0, 0, 0))],
        out_shape=share_shapes + [jax.ShapeDtypeStruct((4, width, DH), BF16)],
        scratch_shapes=[pltpu.VMEM((span, width), BF16), pltpu.VMEM((width, cols), F32)],
        compiler_params=pltpu.CompilerParams(vmem_limit_bytes=32 * 2**20),
        cost_estimate=pl.CostEstimate(
            flops=6 * 2**30, bytes_accessed=16 * 2**20, transcendentals=0
        ),
        name="weight_grads",
    )(*pieces_a, *pieces_b, turned_b, both)


def collect_kernel(slot_ref, filled_ref, a_ref, b_ref, out_ref):
    tile = pl.program_id(0)
    out_ref[...] = jnp.zeros_like(out_ref)
    arrived = slot_ref.shape[0]

    def add_from(ref):
        def one(q, carry):
            @pl.when(filled_ref[q] != 0)
            def _():
                out_ref[slot_ref[q]] += ref[q].astype(F32)

            return carry

        lax.fori_loop(0, arrived, one, 0)

    @pl.when(tile < SPLIT // DH)
    def _():
        add_from(a_ref)

    @pl.when(tile >= SPLIT // DH)
    def _():
        add_from(b_ref)


def collect(slots, filled, arrived_a, arrived_b, pool_count):
    count, rows, _ = arrived_a.shape
    width = arrived_a.shape[2] + arrived_b.shape[2]
    first = SPLIT // DH
    return pl.pallas_call(
        collect_kernel,
        grid_spec=pltpu.PrefetchScalarGridSpec(
            num_scalar_prefetch=2,
            grid=(width // DH,),
            in_specs=[
                pl.BlockSpec((count, rows, DH), lambda i, *_: (0, 0, jnp.minimum(i, first - 1))),
                pl.BlockSpec((count, rows, DH), lambda i, *_: (0, 0, jnp.maximum(i - first, 0))),
            ],
            out_specs=pl.BlockSpec((pool_count, rows, DH), lambda i, *_: (0, 0, i)),
        ),
        out_shape=jax.ShapeDtypeStruct((pool_count, rows, width), F32),
        compiler_params=pltpu.CompilerParams(vmem_limit_bytes=16 * 2**20),
        name="collect",
    )(slots, filled, arrived_a, arrived_b)


def spread_kernel(place_ref, *refs):
    pieces, (key_ref, value_ref), (held_ref,) = refs[:4], refs[4:6], refs[6:]
    x, z = place_ref[0], place_ref[1]
    rows = pieces[0].shape[1]
    for kx in range(4):
        group = lax.rem(x - kx + 4, 4)
        for kz in range(8):
            at = pl.multiple_of(lax.rem(z - kz + 8, 8) * rows, 16)
            held_ref[group, pl.ds(at, rows), :] = pieces[kx][kz].astype(F32)
    key_ref[:, :DH], key_ref[:, DH:] = held_ref[0], held_ref[1]
    value_ref[:, :DH], value_ref[:, DH:] = held_ref[2], held_ref[3]


def reduce_weight_grads(parts, place):
    x, z = place[0], place[1]
    width = parts.shape[1]
    group = lambda k: lax.dynamic_index_in_dim(parts, lax.rem(x + k, 4), 0, keepdims=False)
    by_x = [group(0)] + [lax.ppermute(group(k), "x", shift(4, k)) for k in (1, 3, 2)]
    part = plus(*by_x).astype(BF16).reshape(8, width // 8, DH)
    block = lambda k: lax.dynamic_index_in_dim(part, lax.rem(z + k, 8), 0, keepdims=False)
    by_z = [block(0)] + [lax.ppermute(block(k), "z", shift(8, k)) for k in (1, 7, 2, 6, 3, 5, 4)]
    total = plus(*by_z).astype(BF16)
    column = jnp.stack([total] + [lax.ppermute(total, "z", shift(8, k)) for k in range(1, 8)])
    pieces = [column] + [lax.ppermute(column, "x", shift(4, k)) for k in range(1, 4)]
    shape = jax.ShapeDtypeStruct((width, 2 * DH), F32)
    return pl.pallas_call(
        spread_kernel,
        grid_spec=pltpu.PrefetchScalarGridSpec(
            num_scalar_prefetch=1,
            grid=(1,),
            in_specs=[pl.BlockSpec(p.shape, lambda i, *_: (0, 0, 0)) for p in pieces],
            out_specs=[pl.BlockSpec(shape.shape, lambda i, *_: (0, 0))] * 2,
            scratch_shapes=[pltpu.VMEM((4, width, DH), F32)],
        ),
        out_shape=[shape, shape],
        compiler_params=pltpu.CompilerParams(vmem_limit_bytes=16 * 2**20),
        name="spread",
    )(place, *pieces)


def exchange(array):
    return lax.all_to_all(array, ("z", "x"), split_axis=0, concat_axis=0, tiled=True)


def local(queries, pool, w_key, w_value, out_grad, nb_source, nb_slot, nb_count):
    seq_count = lax.axis_size(("z", "x"))
    seq_index = lax.axis_index(("z", "x"))
    requests = CH_DEV * KNB
    capacity = max(2, 2 * requests // seq_count)
    slot_span = seq_count * capacity
    source_table = nb_source.reshape(seq_count, requests)
    slot_table = nb_slot.reshape(seq_count, requests)
    order_ids = jnp.arange(requests)
    matches = source_table[:, :, None] == source_table[:, None, :]
    before = order_ids[None, :] < order_ids[:, None]
    ranks = jnp.sum(jnp.logical_and(matches, before[None, :, :]), axis=2)
    places = jnp.arange(capacity)
    chosen = jnp.logical_and(
        (source_table == seq_index)[:, :, None], ranks[:, :, None] == places[None, None, :]
    )
    picked_slot = jnp.sum(jnp.where(chosen, slot_table[:, :, None], 0), axis=1).reshape(slot_span)
    filled = jnp.any(chosen, axis=1).reshape(slot_span).astype(jnp.int32)
    own_sources = lax.dynamic_index_in_dim(source_table, seq_index, 0, keepdims=False)
    own_ranks = lax.dynamic_index_in_dim(ranks, seq_index, 0, keepdims=False)
    positions = own_sources * capacity + own_ranks
    back = jnp.sum(
        jnp.where(positions[None, :] == jnp.arange(slot_span)[:, None], order_ids[None, :], 0), axis=1
    )
    counts = lax.dynamic_slice_in_dim(nb_count, seq_index * CH_DEV, CH_DEV)
    place = jnp.stack([lax.axis_index("x"), lax.axis_index("z")]).astype(jnp.int32)
    take = lambda array, index: jnp.take(array, index, axis=0, mode="clip")

    weight = jnp.concatenate([w_key, w_value], axis=1)
    turned = weight.T

    incoming_a = exchange(take(pool[:, :, :SPLIT], picked_slot))
    incoming_b = exchange(take(pool[:, :, SPLIT:], picked_slot))
    pieces_a = gather_pieces(take(incoming_a, positions))
    pieces_b = gather_pieces(take(incoming_b, positions))

    attended, grad_queries, mine_a, other_a, both = attention(
        counts, pieces_a, pieces_b, weight, turned[:, :SPLIT], queries, out_grad
    )
    mine_b, other_b, parts = weight_grads(
        pieces_a, pieces_b, turned[:, SPLIT:], both, weight.shape[0]
    )
    arrived_a = exchange(take(scatter_pieces(mine_a, other_a), back))
    arrived_b = exchange(take(scatter_pieces(mine_b, other_b), back))
    grad_pool = collect(picked_slot, filled, arrived_a, arrived_b, pool.shape[0])
    grad_w_key, grad_w_value = reduce_weight_grads(parts, place)
    return attended, grad_queries, grad_pool, grad_w_key, grad_w_value


def solution(mesh):
    grid = Mesh(mesh.devices.reshape(8, 4, 4, 2), ("z", "x", "y", "core"))
    seq, head = ("z", "x"), ("y", "core")
    return jax.shard_map(
        local,
        mesh=grid,
        in_specs=(
            P(seq, head),
            P(seq, head, None),
            P(None, head),
            P(None, head),
            P(seq, head),
            P(),
            P(),
            P(),
        ),
        out_specs=(
            P(seq, head),
            P(seq, head),
            P(seq, head, None),
            P(None, head),
            P(None, head),
        ),
        check_vma=False,
    )
```

```python
import functools
import math

import jax
import jax.numpy as jnp
from jax import lax
from jax.experimental import pallas as pl
from jax.experimental.pallas import tpu as pltpu
from jax.sharding import Mesh
from jax.sharding import PartitionSpec as P

DH = 128
STRETCH = 64
KNB = 2
CH_DEV = 16
ROWS = 16
PIECES = 8
SPAN = KNB * ROWS * PIECES
HALF = 8
GROUP = 4
F32 = jnp.float32
BF16 = jnp.bfloat16

UP = [(i, (i + 1) % 4) for i in range(4)]
DOWN = [((i + 1) % 4, i) for i in range(4)]
SWAP = [(0, 1), (1, 0)]


def dot(a, b, ca, cb):
    return lax.dot_general(a, b, (((ca,), (cb,)), ((), ())), preferred_element_type=F32)


def shift(size, k):
    return [(i, (i + k) % size) for i in range(size)]


def gather_pieces(own):
    half = own.shape[0] // 2
    below = lax.ppermute(own, "y", UP)
    above = lax.ppermute(own, "y", DOWN)
    far_low = lax.ppermute(below[:half], "y", UP)
    far_high = lax.ppermute(above[half:], "y", DOWN)
    mine = [own, above, below, far_low, far_high]
    return mine + [lax.ppermute(piece, "core", SWAP) for piece in mine]


def plus(*terms):
    total = terms[0].astype(F32)
    for term in terms[1:]:
        total = total + term.astype(F32)
    return total


def scatter_pieces(mine, other):
    swapped = lax.ppermute(other, "core", SWAP)
    half = mine.shape[1] // 2
    far = plus(mine[3], swapped[3]).astype(BF16)
    got_low = lax.ppermute(far[:half], "y", UP)
    got_high = lax.ppermute(far[half:], "y", DOWN)
    up_low = plus(mine[1, :half], swapped[1, :half], got_low).astype(BF16)
    up_high = plus(mine[1, half:], swapped[1, half:]).astype(BF16)
    down_low = plus(mine[2, :half], swapped[2, :half]).astype(BF16)
    down_high = plus(mine[2, half:], swapped[2, half:], got_high).astype(BF16)
    from_below = lax.ppermute(jnp.concatenate([up_low, up_high]), "y", UP)
    from_above = lax.ppermute(jnp.concatenate([down_low, down_high]), "y", DOWN)
    return plus(mine[0], swapped[0], from_below, from_above).astype(BF16)


def fill_rows(step, refs, rows_ref):
    half_steps = HALF // GROUP // 2
    for core in range(2):
        own, above, below, far_low, far_high = refs[core * 5 : core * 5 + 5]

        def put(place, ref):
            for c in range(GROUP):
                at = c * SPAN + (core * 4 + place) * KNB * ROWS
                rows_ref[at : at + KNB * ROWS, :] = ref[c * KNB : (c + 1) * KNB].reshape(
                    KNB * ROWS, ref.shape[2]
                )

        put(0, own)
        put(1, above)
        put(2, below)

        @pl.when(step < half_steps)
        def _():
            put(3, far_low)

        @pl.when(step >= half_steps)
        def _():
            put(3, far_high)


def attention_kernel(first, count_ref, *refs):
    pieces = refs[:10]
    key_weight_ref, value_weight_ref, query_ref, grad_ref = refs[10:14]
    if first:
        begun_ref, rest = None, refs[14:]
    else:
        begun_ref, rest = refs[14], refs[15:]
    attended_ref, grad_query_ref, mine_ref, other_ref, out_ref = rest[:5]
    rows_ref, kv_ref, both_ref = rest[5:8]
    total_ref = out_ref if first else rest[8]
    step = pl.program_id(0)
    local = key_weight_ref.shape[1]
    factor = 1.0 / math.sqrt(DH)
    key_cols, value_cols = slice(0, local), slice(local, 2 * local)
    fill_rows(step, pieces, rows_ref)
    head_of = lax.broadcasted_iota(jnp.int32, (STRETCH, local), 1) < DH
    neighbour = (lax.broadcasted_iota(jnp.int32, (SPAN, 1), 0) // ROWS) % KNB

    def spread_heads(x):
        zero = jnp.zeros_like(x)
        return jnp.concatenate([jnp.where(head_of, x, zero), jnp.where(head_of, zero, x)], axis=0)

    def join_heads(x):
        return jnp.where(head_of, x[:STRETCH], x[STRETCH:])

    stretches = [
        (slice(c * SPAN, (c + 1) * SPAN), slice(c * STRETCH, (c + 1) * STRETCH))
        for c in range(GROUP)
    ]
    for rows, _ in stretches:
        panel = rows_ref[rows, :]
        kv_ref[rows, key_cols] = dot(panel, key_weight_ref[...], 1, 0).astype(BF16)
        kv_ref[rows, value_cols] = dot(panel, value_weight_ref[...], 1, 0).astype(BF16)
    products = []
    for rows, tokens in stretches:
        query, grad = spread_heads(query_ref[tokens, :]), spread_heads(grad_ref[tokens, :])
        scores = dot(kv_ref[rows, key_cols], query, 1, 1) * factor
        dprobs = dot(kv_ref[rows, value_cols], grad, 1, 1)
        products.append((query, grad, scores, dprobs))
    softened = []
    for c in range(GROUP):
        _, _, scores, dprobs = products[c]
        scores = jnp.where(neighbour < count_ref[step * GROUP + c], scores, -jnp.inf)
        powers = jnp.exp(scores - jnp.max(scores, axis=0, keepdims=True))
        probs = powers * (1.0 / jnp.sum(powers, axis=0, keepdims=True))
        row_dot = jnp.sum(probs * dprobs, axis=0, keepdims=True)
        softened.append((probs.astype(BF16), (probs * (dprobs - row_dot)).astype(BF16)))
    for c, (rows, tokens) in enumerate(stretches):
        query, grad, _, _ = products[c]
        weights, dscores = softened[c]
        both_ref[rows, key_cols] = (dot(dscores, query, 1, 0) * factor).astype(BF16)
        both_ref[rows, value_cols] = dot(weights, grad, 1, 0).astype(BF16)
        attended_ref[tokens, :] = join_heads(dot(weights, kv_ref[rows, value_cols], 0, 0)).astype(
            BF16
        )
        grad_query_ref[tokens, :] = (
            join_heads(dot(dscores, kv_ref[rows, key_cols], 0, 0)) * factor
        ).astype(BF16)
    for c, (rows, _) in enumerate(stretches):
        share = dot(both_ref[rows, key_cols], key_weight_ref[...], 1, 1)
        share = share + dot(both_ref[rows, value_cols], value_weight_ref[...], 1, 1)
        share = share.astype(BF16)
        for piece in range(PIECES):
            ref = mine_ref if piece < 4 else other_ref
            at = piece * KNB * ROWS
            ref[piece % 4, c * KNB : (c + 1) * KNB] = share[at : at + KNB * ROWS].reshape(
                KNB, ROWS, share.shape[1]
            )
    part = dot(rows_ref[...], both_ref[...], 0, 0)

    @pl.when(step == 0)
    def _():
        total_ref[...] = part if first else begun_ref[...] + part

    @pl.when(step > 0)
    def _():
        total_ref[...] += part

    if not first:

        @pl.when(step == pl.num_programs(0) - 1)
        def _():
            for g in range(4):
                out_ref[g] = total_ref[:, g * DH : (g + 1) * DH].astype(BF16)


def attention(counts, pieces, w_key, w_value, queries, out_grad, half, begun):
    width, local = w_key.shape
    tokens = HALF * STRETCH
    panels = HALF * KNB
    steps = HALF // GROUP
    half_steps = steps // 2
    first = begun is None
    block = (GROUP * KNB, ROWS, width)
    plain = pl.BlockSpec(block, lambda i, *_: (i, 0, 0))
    low = pl.BlockSpec(block, lambda i, *_: (jnp.minimum(i, half_steps - 1), 0, 0))
    high = pl.BlockSpec(block, lambda i, *_: (jnp.maximum(i - half_steps, 0), 0, 0))
    token_in = pl.BlockSpec((GROUP * STRETCH, local), lambda i, *_: (i + half * steps, 0))
    token_out = pl.BlockSpec((GROUP * STRETCH, local), lambda i, *_: (i, 0))
    share = pl.BlockSpec((4, GROUP * KNB, ROWS, width), lambda i, *_: (0, i, 0, 0))
    whole = lambda shape: pl.BlockSpec(shape, lambda i, *_: (0,) * len(shape))
    total = (width, 2 * local)
    out = jax.ShapeDtypeStruct(total, F32) if first else jax.ShapeDtypeStruct((4, width, DH), BF16)
    token_shape = jax.ShapeDtypeStruct((tokens, local), BF16)
    share_shape = jax.ShapeDtypeStruct((4, panels, ROWS, width), BF16)
    scratch = [
        pltpu.VMEM((GROUP * SPAN, width), BF16),
        pltpu.VMEM((GROUP * SPAN, 2 * local), BF16),
        pltpu.VMEM((GROUP * SPAN, 2 * local), BF16),
    ]
    return pl.pallas_call(
        functools.partial(attention_kernel, first),
        grid_spec=pltpu.PrefetchScalarGridSpec(
            num_scalar_prefetch=1,
            grid=(steps,),
            in_specs=[plain, plain, plain, low, high] * 2
            + [whole(w_key.shape), whole(w_key.shape), token_in, token_in]
            + ([] if first else [whole(total)]),
            out_specs=[token_out, token_out, share, share, whole(out.shape)],
            scratch_shapes=scratch + ([] if first else [pltpu.VMEM(total, F32)]),
        ),
        out_shape=[token_shape, token_shape, share_shape, share_shape, out],
        compiler_params=pltpu.CompilerParams(vmem_limit_bytes=56 * 2**20),
        cost_estimate=pl.CostEstimate(
            flops=8 * 2**30, bytes_accessed=16 * 2**20, transcendentals=2**18
        ),
        name="attention",
    )(counts, *pieces, w_key, w_value, queries, out_grad, *([] if first else [begun]))


def collect_kernel(slot_ref, filled_ref, arrived_ref, out_ref):
    out_ref[...] = jnp.zeros_like(out_ref)

    def one(q, carry):
        @pl.when(filled_ref[q] != 0)
        def _():
            out_ref[slot_ref[q]] += arrived_ref[q].astype(F32)

        return carry

    lax.fori_loop(0, slot_ref.shape[0], one, 0)


def collect(slots, filled, arrived, pool_count):
    count, rows, width = arrived.shape
    return pl.pallas_call(
        collect_kernel,
        grid_spec=pltpu.PrefetchScalarGridSpec(
            num_scalar_prefetch=2,
            grid=(1,),
            in_specs=[pl.BlockSpec((count, rows, width), lambda i, *_: (0, 0, 0))],
            out_specs=pl.BlockSpec((pool_count, rows, width), lambda i, *_: (0, 0, 0)),
        ),
        out_shape=jax.ShapeDtypeStruct((pool_count, rows, width), F32),
        compiler_params=pltpu.CompilerParams(vmem_limit_bytes=16 * 2**20),
        name="collect",
    )(slots, filled, arrived)


def reduce_weight_grads(parts):
    width = parts.shape[1]
    by_x = lax.all_to_all(parts, "x", split_axis=0, concat_axis=0, tiled=True)
    part = plus(*[by_x[k] for k in range(4)]).astype(BF16).reshape(8, width // 8, DH)
    by_z = lax.all_to_all(part, "z", split_axis=0, concat_axis=0, tiled=True)
    total = plus(*[by_z[k] for k in range(8)])
    column = lax.all_gather(total, "z", axis=0, tiled=True)
    groups = lax.all_gather(column, "x", axis=0, tiled=False)
    return (
        jnp.concatenate([groups[0], groups[1]], axis=1),
        jnp.concatenate([groups[2], groups[3]], axis=1),
    )


def exchange(array):
    return lax.all_to_all(array, ("z", "x"), split_axis=0, concat_axis=0, tiled=True)


def local(queries, pool, w_key, w_value, out_grad, nb_source, nb_slot, nb_count):
    seq_count = lax.axis_size(("z", "x"))
    seq_index = lax.axis_index(("z", "x"))
    requests = CH_DEV * KNB
    capacity = max(2, 2 * requests // seq_count)
    slot_span = seq_count * capacity
    source_table = nb_source.reshape(seq_count, requests)
    slot_table = nb_slot.reshape(seq_count, requests)
    order_ids = jnp.arange(requests)
    matches = source_table[:, :, None] == source_table[:, None, :]
    before = order_ids[None, :] < order_ids[:, None]
    ranks = jnp.sum(jnp.logical_and(matches, before[None, :, :]), axis=2)
    places = jnp.arange(capacity)
    chosen = jnp.logical_and(
        (source_table == seq_index)[:, :, None], ranks[:, :, None] == places[None, None, :]
    )
    picked_slot = jnp.sum(jnp.where(chosen, slot_table[:, :, None], 0), axis=1).reshape(slot_span)
    filled = jnp.any(chosen, axis=1).reshape(slot_span).astype(jnp.int32)
    own_sources = lax.dynamic_index_in_dim(source_table, seq_index, 0, keepdims=False)
    own_ranks = lax.dynamic_index_in_dim(ranks, seq_index, 0, keepdims=False)
    positions = own_sources * capacity + own_ranks
    back = jnp.sum(
        jnp.where(positions[None, :] == jnp.arange(slot_span)[:, None], order_ids[None, :], 0), axis=1
    )
    counts = lax.dynamic_slice_in_dim(nb_count, seq_index * CH_DEV, CH_DEV)
    take = lambda array, index: jnp.take(array, index, axis=0, mode="clip")

    incoming = exchange(take(pool, picked_slot))
    begun, attended, grad_queries, summed = None, [], [], []
    panels = HALF * KNB
    pieces = [
        gather_pieces(take(incoming, positions[half * panels : (half + 1) * panels]))
        for half in range(2)
    ]
    for half in range(2):
        attended_half, grad_half, mine, other, begun = attention(
            counts[half * HALF : (half + 1) * HALF],
            pieces[half],
            w_key,
            w_value,
            queries,
            out_grad,
            half,
            begun,
        )
        attended.append(attended_half)
        grad_queries.append(grad_half)
        summed.append(scatter_pieces(mine, other))
    grad_w_key, grad_w_value = reduce_weight_grads(begun)
    arrived = exchange(take(jnp.concatenate(summed), back))
    grad_pool = collect(picked_slot, filled, arrived, pool.shape[0])
    return (
        jnp.concatenate(attended),
        jnp.concatenate(grad_queries),
        grad_pool,
        grad_w_key,
        grad_w_value,
    )


def solution(mesh):
    grid = Mesh(mesh.devices.reshape(8, 4, 4, 2), ("z", "x", "y", "core"))
    seq, head = ("z", "x"), ("y", "core")
    return jax.shard_map(
        local,
        mesh=grid,
        in_specs=(
            P(seq, head),
            P(seq, head, None),
            P(None, head),
            P(None, head),
            P(seq, head),
            P(),
            P(),
            P(),
        ),
        out_specs=(
            P(seq, head),
            P(seq, head),
            P(seq, head, None),
            P(None, head),
            P(None, head),
        ),
        check_vma=False,
    )
```

```python
import functools
import math

import jax
import jax.numpy as jnp
from jax import lax
from jax.experimental import pallas as pl
from jax.experimental.pallas import tpu as pltpu
from jax.sharding import Mesh
from jax.sharding import PartitionSpec as P

DH = 128
STRETCH = 64
KNB = 2
CH_DEV = 16
ROWS = 16
PIECES = 8
SPAN = KNB * ROWS * PIECES
HALF = 8
GROUP = 4
F32 = jnp.float32
BF16 = jnp.bfloat16

UP = [(i, (i + 1) % 4) for i in range(4)]
DOWN = [((i + 1) % 4, i) for i in range(4)]
SWAP = [(0, 1), (1, 0)]


def dot(a, b, ca, cb):
    return lax.dot_general(a, b, (((ca,), (cb,)), ((), ())), preferred_element_type=F32)


def shift(size, k):
    return [(i, (i + k) % size) for i in range(size)]


def gather_pieces(own):
    half = own.shape[0] // 2
    below = lax.ppermute(own, "y", UP)
    above = lax.ppermute(own, "y", DOWN)
    far_low = lax.ppermute(below[:half], "y", UP)
    far_high = lax.ppermute(above[half:], "y", DOWN)
    mine = [own, above, below, far_low, far_high]
    return mine + [lax.ppermute(piece, "core", SWAP) for piece in mine]


def plus(*terms):
    total = terms[0].astype(F32)
    for term in terms[1:]:
        total = total + term.astype(F32)
    return total


def scatter_pieces(mine, other, parts):
    swapped = lax.ppermute(other, "core", SWAP)
    half = mine.shape[1] // 2
    far, parts = lax.optimization_barrier((plus(mine[3], swapped[3]).astype(BF16), parts))
    got_low = lax.ppermute(far[:half], "y", UP)
    got_high = lax.ppermute(far[half:], "y", DOWN)
    up_low = plus(mine[1, :half], swapped[1, :half], got_low).astype(BF16)
    up_high = plus(mine[1, half:], swapped[1, half:]).astype(BF16)
    down_low = plus(mine[2, :half], swapped[2, :half]).astype(BF16)
    down_high = plus(mine[2, half:], swapped[2, half:], got_high).astype(BF16)
    from_below = lax.ppermute(jnp.concatenate([up_low, up_high]), "y", UP)
    from_above = lax.ppermute(jnp.concatenate([down_low, down_high]), "y", DOWN)
    total = plus(mine[0], swapped[0], from_below, from_above).astype(BF16)
    return total, parts, (from_below, total)


def after(value, *others):
    return lax.optimization_barrier((value,) + others)[0]


def fill_from_pieces(step, refs, rows_ref):
    half_steps = HALF // GROUP // 2
    for core in range(2):
        own, above, below, far_low, far_high = refs[core * 5 : core * 5 + 5]

        def put(place, ref):
            for c in range(GROUP):
                at = c * SPAN + (core * 4 + place) * KNB * ROWS
                rows_ref[at : at + KNB * ROWS, :] = ref[c * KNB : (c + 1) * KNB].reshape(
                    KNB * ROWS, ref.shape[2]
                )

        put(0, own)
        put(1, above)
        put(2, below)

        @pl.when(step < half_steps)
        def _():
            put(3, far_low)

        @pl.when(step >= half_steps)
        def _():
            put(3, far_high)


def fill_from_gathered(order_ref, gathered_ref, rows_ref):
    for piece in range(PIECES):
        source = order_ref[piece]
        for c in range(GROUP):
            at = c * SPAN + piece * KNB * ROWS
            rows_ref[at : at + KNB * ROWS, :] = gathered_ref[
                source, c * KNB : (c + 1) * KNB
            ].reshape(KNB * ROWS, gathered_ref.shape[3])


def attention_kernel(first, count_ref, order_ref, *refs):
    step = pl.program_id(0)
    if first:
        pieces, refs = refs[:10], refs[10:]
    else:
        gathered_ref, begun_ref, refs = refs[0], refs[1], refs[2:]
    key_weight_ref, value_weight_ref, query_ref, grad_ref, attended_ref, grad_query_ref = refs[:6]
    refs = refs[6:]
    if first:
        share_ref, out_ref, rows_ref, kv_ref, both_ref = refs
        total_ref = out_ref
        fill_from_pieces(step, pieces, rows_ref)
    else:
        mine_ref, other_ref, out_ref, rows_ref, kv_ref, both_ref, total_ref = refs
        fill_from_gathered(order_ref, gathered_ref, rows_ref)
    local = key_weight_ref.shape[1]
    factor = 1.0 / math.sqrt(DH)
    key_cols, value_cols = slice(0, local), slice(local, 2 * local)
    head_of = lax.broadcasted_iota(jnp.int32, (STRETCH, local), 1) < DH
    neighbour = (lax.broadcasted_iota(jnp.int32, (SPAN, 1), 0) // ROWS) % KNB

    def spread_heads(x):
        zero = jnp.zeros_like(x)
        return jnp.concatenate([jnp.where(head_of, x, zero), jnp.where(head_of, zero, x)], axis=0)

    def join_heads(x):
        return jnp.where(head_of, x[:STRETCH], x[STRETCH:])

    stretches = [
        (slice(c * SPAN, (c + 1) * SPAN), slice(c * STRETCH, (c + 1) * STRETCH))
        for c in range(GROUP)
    ]
    for rows, _ in stretches:
        panel = rows_ref[rows, :]
        kv_ref[rows, key_cols] = dot(panel, key_weight_ref[...], 1, 0).astype(BF16)
        kv_ref[rows, value_cols] = dot(panel, value_weight_ref[...], 1, 0).astype(BF16)
    products = []
    for rows, tokens in stretches:
        query, grad = spread_heads(query_ref[tokens, :]), spread_heads(grad_ref[tokens, :])
        scores = dot(kv_ref[rows, key_cols], query, 1, 1) * factor
        dprobs = dot(kv_ref[rows, value_cols], grad, 1, 1)
        products.append((query, grad, scores, dprobs))
    softened = []
    for c in range(GROUP):
        _, _, scores, dprobs = products[c]
        scores = jnp.where(neighbour < count_ref[step * GROUP + c], scores, -jnp.inf)
        powers = jnp.exp(scores - jnp.max(scores, axis=0, keepdims=True))
        probs = powers * (1.0 / jnp.sum(powers, axis=0, keepdims=True))
        row_dot = jnp.sum(probs * dprobs, axis=0, keepdims=True)
        softened.append((probs.astype(BF16), (probs * (dprobs - row_dot)).astype(BF16)))
    for c, (rows, tokens) in enumerate(stretches):
        query, grad, _, _ = products[c]
        weights, dscores = softened[c]
        both_ref[rows, key_cols] = (dot(dscores, query, 1, 0) * factor).astype(BF16)
        both_ref[rows, value_cols] = dot(weights, grad, 1, 0).astype(BF16)
        attended_ref[tokens, :] = join_heads(dot(weights, kv_ref[rows, value_cols], 0, 0)).astype(
            BF16
        )
        grad_query_ref[tokens, :] = (
            join_heads(dot(dscores, kv_ref[rows, key_cols], 0, 0)) * factor
        ).astype(BF16)
    for c, (rows, _) in enumerate(stretches):
        share = dot(both_ref[rows, key_cols], key_weight_ref[...], 1, 1)
        share = share + dot(both_ref[rows, value_cols], value_weight_ref[...], 1, 1)
        share = share.astype(BF16)
        for piece in range(PIECES):
            at = piece * KNB * ROWS
            part = share[at : at + KNB * ROWS].reshape(KNB, ROWS, share.shape[1])
            panels = slice(c * KNB, (c + 1) * KNB)
            if first:
                share_ref[order_ref[piece], panels] = part
            elif piece < 4:
                mine_ref[piece, panels] = part
            else:
                other_ref[piece - 4, panels] = part
    part = dot(rows_ref[...], both_ref[...], 0, 0)

    @pl.when(step == 0)
    def _():
        total_ref[...] = part if first else begun_ref[...] + part

    @pl.when(step > 0)
    def _():
        total_ref[...] += part

    if not first:

        @pl.when(step == pl.num_programs(0) - 1)
        def _():
            for g in range(4):
                out_ref[g] = total_ref[:, g * DH : (g + 1) * DH].astype(BF16)


def attention(counts, order, panels, w_key, w_value, queries, out_grad, half, begun):
    width, local = w_key.shape
    tokens = HALF * STRETCH
    steps = HALF // GROUP
    half_steps = steps // 2
    first = begun is None
    block = (GROUP * KNB, ROWS, width)
    plain = pl.BlockSpec(block, lambda i, *_: (i, 0, 0))
    low = pl.BlockSpec(block, lambda i, *_: (jnp.minimum(i, half_steps - 1), 0, 0))
    high = pl.BlockSpec(block, lambda i, *_: (jnp.maximum(i - half_steps, 0), 0, 0))
    stacked = lambda n: pl.BlockSpec((n,) + block, lambda i, *_: (0, i, 0, 0))
    stacked_shape = lambda n: jax.ShapeDtypeStruct((n, HALF * KNB, ROWS, width), BF16)
    token_in = pl.BlockSpec((GROUP * STRETCH, local), lambda i, *_: (i + half * steps, 0))
    token_out = pl.BlockSpec((GROUP * STRETCH, local), lambda i, *_: (i, 0))
    token_shape = jax.ShapeDtypeStruct((tokens, local), BF16)
    whole = lambda shape: pl.BlockSpec(shape, lambda i, *_: (0,) * len(shape))
    total = (width, 2 * local)
    scratch = [
        pltpu.VMEM((GROUP * SPAN, width), BF16),
        pltpu.VMEM((GROUP * SPAN, 2 * local), BF16),
        pltpu.VMEM((GROUP * SPAN, 2 * local), BF16),
    ]
    if first:
        in_specs = [plain, plain, plain, low, high] * 2
        share_specs, share_shapes = [stacked(PIECES)], [stacked_shape(PIECES)]
        out = jax.ShapeDtypeStruct(total, F32)
    else:
        in_specs = [stacked(PIECES), whole(total)]
        panels = [panels, begun]
        share_specs, share_shapes = [stacked(4)] * 2, [stacked_shape(4)] * 2
        out = jax.ShapeDtypeStruct((4, width, DH), BF16)
        scratch = scratch + [pltpu.VMEM(total, F32)]
    return pl.pallas_call(
        functools.partial(attention_kernel, first),
        grid_spec=pltpu.PrefetchScalarGridSpec(
            num_scalar_prefetch=2,
            grid=(steps,),
            in_specs=in_specs + [whole(w_key.shape), whole(w_key.shape), token_in, token_in],
            out_specs=[token_out, token_out] + share_specs + [whole(out.shape)],
            scratch_shapes=scratch,
        ),
        out_shape=[token_shape, token_shape] + share_shapes + [out],
        compiler_params=pltpu.CompilerParams(vmem_limit_bytes=56 * 2**20),
        cost_estimate=pl.CostEstimate(
            flops=8 * 2**30, bytes_accessed=16 * 2**20, transcendentals=2**18
        ),
        name="attention",
    )(counts, order, *panels, w_key, w_value, queries, out_grad)


def collect_kernel(slot_ref, filled_ref, arrived_ref, out_ref):
    out_ref[...] = jnp.zeros_like(out_ref)

    def one(q, carry):
        @pl.when(filled_ref[q] != 0)
        def _():
            out_ref[slot_ref[q]] += arrived_ref[q].astype(F32)

        return carry

    lax.fori_loop(0, slot_ref.shape[0], one, 0)


def collect(slots, filled, arrived, pool_count):
    count, rows, width = arrived.shape
    return pl.pallas_call(
        collect_kernel,
        grid_spec=pltpu.PrefetchScalarGridSpec(
            num_scalar_prefetch=2,
            grid=(1,),
            in_specs=[pl.BlockSpec((count, rows, width), lambda i, *_: (0, 0, 0))],
            out_specs=pl.BlockSpec((pool_count, rows, width), lambda i, *_: (0, 0, 0)),
        ),
        out_shape=jax.ShapeDtypeStruct((pool_count, rows, width), F32),
        compiler_params=pltpu.CompilerParams(vmem_limit_bytes=16 * 2**20),
        name="collect",
    )(slots, filled, arrived)


def reduce_weight_grads(parts, stages):
    width = parts.shape[1]
    by_x = lax.all_to_all(parts, "x", split_axis=0, concat_axis=0, tiled=True)
    part = plus(*[by_x[k] for k in range(4)]).astype(BF16).reshape(8, width // 8, DH)
    by_z = lax.all_to_all(part, "z", split_axis=0, concat_axis=0, tiled=True)
    by_z = after(by_z, stages[0])
    total = plus(*[by_z[k] for k in range(8)]).astype(BF16)
    column = jnp.broadcast_to(total[None], part.shape)
    column = lax.all_to_all(column, "z", split_axis=0, concat_axis=0, tiled=True)
    column = after(column, stages[1])
    groups = jnp.broadcast_to(column.reshape(width, DH)[None], parts.shape)
    groups = lax.all_to_all(groups, "x", split_axis=0, concat_axis=0, tiled=True).astype(F32)
    return (
        jnp.concatenate([groups[0], groups[1]], axis=1),
        jnp.concatenate([groups[2], groups[3]], axis=1),
    )


def exchange(array):
    return lax.all_to_all(array, ("z", "x"), split_axis=0, concat_axis=0, tiled=True)


def local(queries, pool, w_key, w_value, out_grad, nb_source, nb_slot, nb_count):
    seq_count = lax.axis_size(("z", "x"))
    seq_index = lax.axis_index(("z", "x"))
    requests = CH_DEV * KNB
    capacity = max(2, 2 * requests // seq_count)
    slot_span = seq_count * capacity
    source_table = nb_source.reshape(seq_count, requests)
    slot_table = nb_slot.reshape(seq_count, requests)
    order_ids = jnp.arange(requests)
    matches = source_table[:, :, None] == source_table[:, None, :]
    before = order_ids[None, :] < order_ids[:, None]
    ranks = jnp.sum(jnp.logical_and(matches, before[None, :, :]), axis=2)
    places = jnp.arange(capacity)
    chosen = jnp.logical_and(
        (source_table == seq_index)[:, :, None], ranks[:, :, None] == places[None, None, :]
    )
    picked_slot = jnp.sum(jnp.where(chosen, slot_table[:, :, None], 0), axis=1).reshape(slot_span)
    filled = jnp.any(chosen, axis=1).reshape(slot_span).astype(jnp.int32)
    own_sources = lax.dynamic_index_in_dim(source_table, seq_index, 0, keepdims=False)
    own_ranks = lax.dynamic_index_in_dim(ranks, seq_index, 0, keepdims=False)
    positions = own_sources * capacity + own_ranks
    back = jnp.sum(
        jnp.where(positions[None, :] == jnp.arange(slot_span)[:, None], order_ids[None, :], 0), axis=1
    )
    counts = lax.dynamic_slice_in_dim(nb_count, seq_index * CH_DEV, CH_DEV)
    take = lambda array, index: jnp.take(array, index, axis=0, mode="clip")

    incoming = exchange(take(pool, picked_slot))
    y, core = lax.axis_index("y"), lax.axis_index("core")
    order = jnp.stack(
        [(y + dy) % 4 * 2 + (core + other) % 2 for other in (0, 1) for dy in (0, 1, 3, 2)]
    ).astype(jnp.int32)
    panels = HALF * KNB
    wanted = take(incoming, positions)
    pieces = gather_pieces(wanted[:panels])
    gathered = lax.all_gather(wanted[panels:], ("y", "core"), axis=0)
    weights = (w_key, w_value, queries, out_grad)
    attended_0, grad_queries_0, share, begun = attention(
        counts[:HALF], order, pieces, *weights, 0, None
    )
    summed_0 = lax.psum_scatter(share, ("y", "core"), scatter_dimension=0)
    attended_1, grad_queries_1, mine, other, parts = attention(
        counts[HALF:], order, gathered, *weights, 1, begun
    )
    summed_1, parts, stages = scatter_pieces(mine, other, parts)
    grad_w_key, grad_w_value = reduce_weight_grads(parts, stages)
    arrived = exchange(take(jnp.concatenate([summed_0, summed_1]), back))
    grad_pool = collect(picked_slot, filled, arrived, pool.shape[0])
    return (
        jnp.concatenate([attended_0, attended_1]),
        jnp.concatenate([grad_queries_0, grad_queries_1]),
        grad_pool,
        grad_w_key,
        grad_w_value,
    )


def solution(mesh):
    grid = Mesh(mesh.devices.reshape(8, 4, 4, 2), ("z", "x", "y", "core"))
    seq, head = ("z", "x"), ("y", "core")
    return jax.shard_map(
        local,
        mesh=grid,
        in_specs=(
            P(seq, head),
            P(seq, head, None),
            P(None, head),
            P(None, head),
            P(seq, head),
            P(),
            P(),
            P(),
        ),
        out_specs=(
            P(seq, head),
            P(seq, head),
            P(seq, head, None),
            P(None, head),
            P(None, head),
        ),
        check_vma=False,
    )
```

```python
import functools
import math

import jax
import jax.numpy as jnp
from jax import lax
from jax.experimental import pallas as pl
from jax.experimental.pallas import tpu as pltpu
from jax.sharding import Mesh
from jax.sharding import PartitionSpec as P

DH = 128
STRETCH = 64
KNB = 2
CH_DEV = 16
ROWS = 16
PIECES = 8
SPAN = KNB * ROWS * PIECES
HALF = 8
GROUP = 4
F32 = jnp.float32
BF16 = jnp.bfloat16

UP = [(i, (i + 1) % 4) for i in range(4)]
DOWN = [((i + 1) % 4, i) for i in range(4)]
SWAP = [(0, 1), (1, 0)]


def dot(a, b, ca, cb):
    return lax.dot_general(a, b, (((ca,), (cb,)), ((), ())), preferred_element_type=F32)


def shift(size, k):
    return [(i, (i + k) % size) for i in range(size)]


def gather_pieces(own):
    half = own.shape[0] // 2
    below = lax.ppermute(own, "y", UP)
    above = lax.ppermute(own, "y", DOWN)
    far_low = lax.ppermute(below[:half], "y", UP)
    far_high = lax.ppermute(above[half:], "y", DOWN)
    mine = [own, above, below, far_low, far_high]
    return mine + [lax.ppermute(piece, "core", SWAP) for piece in mine]


def plus(*terms):
    total = terms[0].astype(F32)
    for term in terms[1:]:
        total = total + term.astype(F32)
    return total


def scatter_and_reduce(mine, other, parts):
    half = mine.shape[1] // 2
    swapped = lax.ppermute(other, "core", SWAP)
    by_x = lax.all_to_all(parts, "x", split_axis=0, concat_axis=0, tiled=True)
    part = plus(*[by_x[k] for k in range(4)]).astype(BF16).reshape(8, -1, DH)
    far = plus(mine[3], swapped[3]).astype(BF16)
    far, part = lax.optimization_barrier((far, part))
    got_low = lax.ppermute(far[:half], "y", UP)
    got_high = lax.ppermute(far[half:], "y", DOWN)
    by_z = lax.all_to_all(part, "z", split_axis=0, concat_axis=0, tiled=True)
    up_low = plus(mine[1, :half], swapped[1, :half], got_low).astype(BF16)
    up_high = plus(mine[1, half:], swapped[1, half:]).astype(BF16)
    down_low = plus(mine[2, :half], swapped[2, :half]).astype(BF16)
    down_high = plus(mine[2, half:], swapped[2, half:], got_high).astype(BF16)
    up = jnp.concatenate([up_low, up_high])
    down = jnp.concatenate([down_low, down_high])
    total = plus(*[by_z[k] for k in range(8)]).astype(BF16)
    up, down, total = lax.optimization_barrier((up, down, total))
    from_below = lax.ppermute(up, "y", UP)
    from_above = lax.ppermute(down, "y", DOWN)
    column = jnp.broadcast_to(total[None], part.shape)
    column = lax.all_to_all(column, "z", split_axis=0, concat_axis=0, tiled=True)
    summed = plus(mine[0], swapped[0], from_below, from_above).astype(BF16)
    return summed, column.reshape(-1, DH)


def fill_from_pieces(step, refs, rows_ref):
    half_steps = HALF // GROUP // 2
    for core in range(2):
        own, above, below, far_low, far_high = refs[core * 5 : core * 5 + 5]

        def put(place, ref):
            for c in range(GROUP):
                at = c * SPAN + (core * 4 + place) * KNB * ROWS
                rows_ref[at : at + KNB * ROWS, :] = ref[c * KNB : (c + 1) * KNB].reshape(
                    KNB * ROWS, ref.shape[2]
                )

        put(0, own)
        put(1, above)
        put(2, below)

        @pl.when(step < half_steps)
        def _():
            put(3, far_low)

        @pl.when(step >= half_steps)
        def _():
            put(3, far_high)


def fill_from_gathered(order_ref, gathered_ref, rows_ref):
    for piece in range(PIECES):
        source = order_ref[piece]
        for c in range(GROUP):
            at = c * SPAN + piece * KNB * ROWS
            rows_ref[at : at + KNB * ROWS, :] = gathered_ref[
                source, c * KNB : (c + 1) * KNB
            ].reshape(KNB * ROWS, gathered_ref.shape[3])


def attention_kernel(first, count_ref, order_ref, *refs):
    step = pl.program_id(0)
    if first:
        pieces, refs = refs[:10], refs[10:]
    else:
        gathered_ref, begun_ref, refs = refs[0], refs[1], refs[2:]
    key_weight_ref, value_weight_ref, query_ref, grad_ref, attended_ref, grad_query_ref = refs[:6]
    refs = refs[6:]
    if first:
        share_ref, out_ref, rows_ref, kv_ref, both_ref = refs
        total_ref = out_ref
        fill_from_pieces(step, pieces, rows_ref)
    else:
        mine_ref, other_ref, out_ref, rows_ref, kv_ref, both_ref, total_ref = refs
        fill_from_gathered(order_ref, gathered_ref, rows_ref)
    local = key_weight_ref.shape[1]
    factor = 1.0 / math.sqrt(DH)
    key_cols, value_cols = slice(0, local), slice(local, 2 * local)
    head_of = lax.broadcasted_iota(jnp.int32, (STRETCH, local), 1) < DH
    neighbour = (lax.broadcasted_iota(jnp.int32, (SPAN, 1), 0) // ROWS) % KNB

    def spread_heads(x):
        zero = jnp.zeros_like(x)
        return jnp.concatenate([jnp.where(head_of, x, zero), jnp.where(head_of, zero, x)], axis=0)

    def join_heads(x):
        return jnp.where(head_of, x[:STRETCH], x[STRETCH:])

    stretches = [
        (slice(c * SPAN, (c + 1) * SPAN), slice(c * STRETCH, (c + 1) * STRETCH))
        for c in range(GROUP)
    ]
    for rows, _ in stretches:
        panel = rows_ref[rows, :]
        kv_ref[rows, key_cols] = dot(panel, key_weight_ref[...], 1, 0).astype(BF16)
        kv_ref[rows, value_cols] = dot(panel, value_weight_ref[...], 1, 0).astype(BF16)
    products = []
    for rows, tokens in stretches:
        query, grad = spread_heads(query_ref[tokens, :]), spread_heads(grad_ref[tokens, :])
        scores = dot(kv_ref[rows, key_cols], query, 1, 1) * factor
        dprobs = dot(kv_ref[rows, value_cols], grad, 1, 1)
        products.append((query, grad, scores, dprobs))
    softened = []
    for c in range(GROUP):
        _, _, scores, dprobs = products[c]
        scores = jnp.where(neighbour < count_ref[step * GROUP + c], scores, -jnp.inf)
        powers = jnp.exp(scores - jnp.max(scores, axis=0, keepdims=True))
        probs = powers * (1.0 / jnp.sum(powers, axis=0, keepdims=True))
        row_dot = jnp.sum(probs * dprobs, axis=0, keepdims=True)
        softened.append((probs.astype(BF16), (probs * (dprobs - row_dot)).astype(BF16)))
    for c, (rows, tokens) in enumerate(stretches):
        query, grad, _, _ = products[c]
        weights, dscores = softened[c]
        both_ref[rows, key_cols] = (dot(dscores, query, 1, 0) * factor).astype(BF16)
        both_ref[rows, value_cols] = dot(weights, grad, 1, 0).astype(BF16)
        attended_ref[tokens, :] = join_heads(dot(weights, kv_ref[rows, value_cols], 0, 0)).astype(
            BF16
        )
        grad_query_ref[tokens, :] = (
            join_heads(dot(dscores, kv_ref[rows, key_cols], 0, 0)) * factor
        ).astype(BF16)
    for c, (rows, _) in enumerate(stretches):
        share = dot(both_ref[rows, key_cols], key_weight_ref[...], 1, 1)
        share = share + dot(both_ref[rows, value_cols], value_weight_ref[...], 1, 1)
        share = share.astype(BF16)
        for piece in range(PIECES):
            at = piece * KNB * ROWS
            part = share[at : at + KNB * ROWS].reshape(KNB, ROWS, share.shape[1])
            panels = slice(c * KNB, (c + 1) * KNB)
            if first:
                share_ref[order_ref[piece], panels] = part
            elif piece < 4:
                mine_ref[piece, panels] = part
            else:
                other_ref[piece - 4, panels] = part
    part = dot(rows_ref[...], both_ref[...], 0, 0)

    @pl.when(step == 0)
    def _():
        total_ref[...] = part if first else begun_ref[...] + part

    @pl.when(step > 0)
    def _():
        total_ref[...] += part

    if not first:

        @pl.when(step == pl.num_programs(0) - 1)
        def _():
            for g in range(4):
                out_ref[g] = total_ref[:, g * DH : (g + 1) * DH].astype(BF16)


def attention(counts, order, panels, w_key, w_value, queries, out_grad, half, begun):
    width, local = w_key.shape
    tokens = HALF * STRETCH
    steps = HALF // GROUP
    half_steps = steps // 2
    first = begun is None
    block = (GROUP * KNB, ROWS, width)
    plain = pl.BlockSpec(block, lambda i, *_: (i, 0, 0))
    low = pl.BlockSpec(block, lambda i, *_: (jnp.minimum(i, half_steps - 1), 0, 0))
    high = pl.BlockSpec(block, lambda i, *_: (jnp.maximum(i - half_steps, 0), 0, 0))
    stacked = lambda n: pl.BlockSpec((n,) + block, lambda i, *_: (0, i, 0, 0))
    stacked_shape = lambda n: jax.ShapeDtypeStruct((n, HALF * KNB, ROWS, width), BF16)
    token_in = pl.BlockSpec((GROUP * STRETCH, local), lambda i, *_: (i + half * steps, 0))
    token_out = pl.BlockSpec((GROUP * STRETCH, local), lambda i, *_: (i, 0))
    token_shape = jax.ShapeDtypeStruct((tokens, local), BF16)
    whole = lambda shape: pl.BlockSpec(shape, lambda i, *_: (0,) * len(shape))
    total = (width, 2 * local)
    scratch = [
        pltpu.VMEM((GROUP * SPAN, width), BF16),
        pltpu.VMEM((GROUP * SPAN, 2 * local), BF16),
        pltpu.VMEM((GROUP * SPAN, 2 * local), BF16),
    ]
    if first:
        in_specs = [plain, plain, plain, low, high] * 2
        share_specs, share_shapes = [stacked(PIECES)], [stacked_shape(PIECES)]
        out = jax.ShapeDtypeStruct(total, F32)
    else:
        in_specs = [stacked(PIECES), whole(total)]
        panels = [panels, begun]
        share_specs, share_shapes = [stacked(4)] * 2, [stacked_shape(4)] * 2
        out = jax.ShapeDtypeStruct((4, width, DH), BF16)
        scratch = scratch + [pltpu.VMEM(total, F32)]
    return pl.pallas_call(
        functools.partial(attention_kernel, first),
        grid_spec=pltpu.PrefetchScalarGridSpec(
            num_scalar_prefetch=2,
            grid=(steps,),
            in_specs=in_specs + [whole(w_key.shape), whole(w_key.shape), token_in, token_in],
            out_specs=[token_out, token_out] + share_specs + [whole(out.shape)],
            scratch_shapes=scratch,
        ),
        out_shape=[token_shape, token_shape] + share_shapes + [out],
        compiler_params=pltpu.CompilerParams(vmem_limit_bytes=56 * 2**20),
        cost_estimate=pl.CostEstimate(
            flops=8 * 2**30, bytes_accessed=16 * 2**20, transcendentals=2**18
        ),
        name="attention",
    )(counts, order, *panels, w_key, w_value, queries, out_grad)


def collect_kernel(slot_ref, filled_ref, arrived_ref, out_ref):
    out_ref[...] = jnp.zeros_like(out_ref)

    def one(q, carry):
        @pl.when(filled_ref[q] != 0)
        def _():
            out_ref[slot_ref[q]] += arrived_ref[q].astype(F32)

        return carry

    lax.fori_loop(0, slot_ref.shape[0], one, 0)


def collect(slots, filled, arrived, pool_count):
    count, rows, width = arrived.shape
    return pl.pallas_call(
        collect_kernel,
        grid_spec=pltpu.PrefetchScalarGridSpec(
            num_scalar_prefetch=2,
            grid=(1,),
            in_specs=[pl.BlockSpec((count, rows, width), lambda i, *_: (0, 0, 0))],
            out_specs=pl.BlockSpec((pool_count, rows, width), lambda i, *_: (0, 0, 0)),
        ),
        out_shape=jax.ShapeDtypeStruct((pool_count, rows, width), F32),
        compiler_params=pltpu.CompilerParams(vmem_limit_bytes=16 * 2**20),
        name="collect",
    )(slots, filled, arrived)


def spread_kernel(place_ref, *refs):
    pieces, (key_ref, value_ref, held_ref) = refs[:4], refs[4:]
    for k in range(4):
        held_ref[lax.rem(place_ref[0] - k + 4, 4)] = pieces[k][...].astype(F32)
    key_ref[:, :DH], key_ref[:, DH:] = held_ref[0], held_ref[1]
    value_ref[:, :DH], value_ref[:, DH:] = held_ref[2], held_ref[3]


def spread_columns(column, place):
    width = column.shape[0]
    pieces = [column] + [lax.ppermute(column, "x", shift(4, k)) for k in (1, 3, 2)]
    pieces = [pieces[0], pieces[1], pieces[3], pieces[2]]
    shape = jax.ShapeDtypeStruct((width, 2 * DH), F32)
    return pl.pallas_call(
        spread_kernel,
        grid_spec=pltpu.PrefetchScalarGridSpec(
            num_scalar_prefetch=1,
            grid=(1,),
            in_specs=[pl.BlockSpec(column.shape, lambda i, *_: (0, 0))] * 4,
            out_specs=[pl.BlockSpec(shape.shape, lambda i, *_: (0, 0))] * 2,
            scratch_shapes=[pltpu.VMEM((4, width, DH), F32)],
        ),
        out_shape=[shape, shape],
        compiler_params=pltpu.CompilerParams(vmem_limit_bytes=16 * 2**20),
        name="spread",
    )(place, *pieces)


def exchange(array):
    return lax.all_to_all(array, ("z", "x"), split_axis=0, concat_axis=0, tiled=True)


def local(queries, pool, w_key, w_value, out_grad, nb_source, nb_slot, nb_count):
    seq_count = lax.axis_size(("z", "x"))
    seq_index = lax.axis_index(("z", "x"))
    requests = CH_DEV * KNB
    capacity = max(2, 2 * requests // seq_count)
    slot_span = seq_count * capacity
    source_table = nb_source.reshape(seq_count, requests)
    slot_table = nb_slot.reshape(seq_count, requests)
    order_ids = jnp.arange(requests)
    matches = source_table[:, :, None] == source_table[:, None, :]
    before = order_ids[None, :] < order_ids[:, None]
    ranks = jnp.sum(jnp.logical_and(matches, before[None, :, :]), axis=2)
    places = jnp.arange(capacity)
    chosen = jnp.logical_and(
        (source_table == seq_index)[:, :, None], ranks[:, :, None] == places[None, None, :]
    )
    picked_slot = jnp.sum(jnp.where(chosen, slot_table[:, :, None], 0), axis=1).reshape(slot_span)
    filled = jnp.any(chosen, axis=1).reshape(slot_span).astype(jnp.int32)
    own_sources = lax.dynamic_index_in_dim(source_table, seq_index, 0, keepdims=False)
    own_ranks = lax.dynamic_index_in_dim(ranks, seq_index, 0, keepdims=False)
    positions = own_sources * capacity + own_ranks
    back = jnp.sum(
        jnp.where(positions[None, :] == jnp.arange(slot_span)[:, None], order_ids[None, :], 0), axis=1
    )
    counts = lax.dynamic_slice_in_dim(nb_count, seq_index * CH_DEV, CH_DEV)
    take = lambda array, index: jnp.take(array, index, axis=0, mode="clip")

    incoming = exchange(take(pool, picked_slot))
    y, core = lax.axis_index("y"), lax.axis_index("core")
    order = jnp.stack(
        [(y + dy) % 4 * 2 + (core + other) % 2 for other in (0, 1) for dy in (0, 1, 3, 2)]
    ).astype(jnp.int32)
    place = lax.axis_index("x").astype(jnp.int32).reshape(1)
    positions, back, counts, order, filled, place = lax.optimization_barrier(
        (positions, back, counts, order, filled, place)
    )
    panels = HALF * KNB
    pieces = gather_pieces(take(incoming, positions[:panels]))
    gathered = lax.all_gather(take(incoming, positions[panels:]), ("y", "core"), axis=0)
    weights = (w_key, w_value, queries, out_grad)
    attended_0, grad_queries_0, share, begun = attention(
        counts[:HALF], order, pieces, *weights, 0, None
    )
    summed_0 = lax.psum_scatter(share, ("y", "core"), scatter_dimension=0)
    attended_1, grad_queries_1, mine, other, parts = attention(
        counts[HALF:], order, gathered, *weights, 1, begun
    )
    summed_1, column = scatter_and_reduce(mine, other, parts)
    returning = take(jnp.concatenate([summed_0, summed_1]), back)
    returning, column = lax.optimization_barrier((returning, column))
    arrived = exchange(returning)
    grad_w_key, grad_w_value = spread_columns(column, place)
    grad_pool = collect(picked_slot, filled, arrived, pool.shape[0])
    return (
        jnp.concatenate([attended_0, attended_1]),
        jnp.concatenate([grad_queries_0, grad_queries_1]),
        grad_pool,
        grad_w_key,
        grad_w_value,
    )


def solution(mesh):
    grid = Mesh(mesh.devices.reshape(8, 4, 4, 2), ("z", "x", "y", "core"))
    seq, head = ("z", "x"), ("y", "core")
    return jax.shard_map(
        local,
        mesh=grid,
        in_specs=(
            P(seq, head),
            P(seq, head, None),
            P(None, head),
            P(None, head),
            P(seq, head),
            P(),
            P(),
            P(),
        ),
        out_specs=(
            P(seq, head),
            P(seq, head),
            P(seq, head, None),
            P(None, head),
            P(None, head),
        ),
        check_vma=False,
    )
```

```python
import functools
import math

import jax
import jax.numpy as jnp
from jax import lax
from jax.experimental import pallas as pl
from jax.experimental.pallas import tpu as pltpu
from jax.sharding import Mesh
from jax.sharding import PartitionSpec as P

DH = 128
STRETCH = 64
KNB = 2
CH_DEV = 16
ROWS = 16
PIECES = 8
SPAN = KNB * ROWS * PIECES
HALF = 8
GROUP = 4
F32 = jnp.float32
BF16 = jnp.bfloat16

UP = [(i, (i + 1) % 4) for i in range(4)]
DOWN = [((i + 1) % 4, i) for i in range(4)]
SWAP = [(0, 1), (1, 0)]


def dot(a, b, ca, cb):
    return lax.dot_general(a, b, (((ca,), (cb,)), ((), ())), preferred_element_type=F32)


def shift(size, k):
    return [(i, (i + k) % size) for i in range(size)]


def gather_pieces(own):
    half = own.shape[0] // 2
    below = lax.ppermute(own, "y", UP)
    above = lax.ppermute(own, "y", DOWN)
    far_low = lax.ppermute(below[:half], "y", UP)
    far_high = lax.ppermute(above[half:], "y", DOWN)
    mine = [own, above, below, far_low, far_high]
    return mine + [lax.ppermute(piece, "core", SWAP) for piece in mine]


def plus(*terms):
    total = terms[0].astype(F32)
    for term in terms[1:]:
        total = total + term.astype(F32)
    return total


def reduce_weight_grads(parts):
    by_x = lax.all_to_all(parts, "x", split_axis=0, concat_axis=0, tiled=True)
    part = plus(*[by_x[k] for k in range(4)]).astype(BF16).reshape(8, -1, DH)
    by_z = lax.all_to_all(part, "z", split_axis=0, concat_axis=0, tiled=True)
    total = plus(*[by_z[k] for k in range(8)]).astype(BF16)
    column = jnp.broadcast_to(total[None], part.shape)
    column = lax.all_to_all(column, "z", split_axis=0, concat_axis=0, tiled=True)
    return column.reshape(-1, DH)


def fill_from_pieces(step, refs, rows_ref):
    half_steps = HALF // GROUP // 2
    for core in range(2):
        own, above, below, far_low, far_high = refs[core * 5 : core * 5 + 5]

        def put(place, ref):
            for c in range(GROUP):
                at = c * SPAN + (core * 4 + place) * KNB * ROWS
                rows_ref[at : at + KNB * ROWS, :] = ref[c * KNB : (c + 1) * KNB].reshape(
                    KNB * ROWS, ref.shape[2]
                )

        put(0, own)
        put(1, above)
        put(2, below)

        @pl.when(step < half_steps)
        def _():
            put(3, far_low)

        @pl.when(step >= half_steps)
        def _():
            put(3, far_high)


def fill_from_gathered(gathered_ref, rows_ref):
    for piece in range(PIECES):
        for c in range(GROUP):
            at = c * SPAN + piece * KNB * ROWS
            rows_ref[at : at + KNB * ROWS, :] = gathered_ref[
                piece, c * KNB : (c + 1) * KNB
            ].reshape(KNB * ROWS, gathered_ref.shape[3])


def attention_kernel(first, count_ref, order_ref, *refs):
    step = pl.program_id(0)
    if first:
        pieces, refs = refs[:10], refs[10:]
    else:
        gathered_ref, begun_ref, _, refs = refs[0], refs[1], refs[2], refs[3:]
    key_weight_ref, value_weight_ref, query_ref, grad_ref, attended_ref, grad_query_ref = refs[:6]
    refs = refs[6:]
    share_ref, out_ref, rows_ref, kv_ref, both_ref = refs[:5]
    if first:
        total_ref = out_ref
        fill_from_pieces(step, pieces, rows_ref)
    else:
        total_ref = refs[5]
        fill_from_gathered(gathered_ref, rows_ref)
    local = key_weight_ref.shape[1]
    factor = 1.0 / math.sqrt(DH)
    key_cols, value_cols = slice(0, local), slice(local, 2 * local)
    head_of = lax.broadcasted_iota(jnp.int32, (STRETCH, local), 1) < DH
    neighbour = (lax.broadcasted_iota(jnp.int32, (SPAN, 1), 0) // ROWS) % KNB

    def spread_heads(x):
        zero = jnp.zeros_like(x)
        return jnp.concatenate([jnp.where(head_of, x, zero), jnp.where(head_of, zero, x)], axis=0)

    def join_heads(x):
        return jnp.where(head_of, x[:STRETCH], x[STRETCH:])

    stretches = [
        (slice(c * SPAN, (c + 1) * SPAN), slice(c * STRETCH, (c + 1) * STRETCH))
        for c in range(GROUP)
    ]
    for rows, _ in stretches:
        panel = rows_ref[rows, :]
        kv_ref[rows, key_cols] = dot(panel, key_weight_ref[...], 1, 0).astype(BF16)
        kv_ref[rows, value_cols] = dot(panel, value_weight_ref[...], 1, 0).astype(BF16)
    products = []
    for rows, tokens in stretches:
        query, grad = spread_heads(query_ref[tokens, :]), spread_heads(grad_ref[tokens, :])
        scores = dot(kv_ref[rows, key_cols], query, 1, 1) * factor
        dprobs = dot(kv_ref[rows, value_cols], grad, 1, 1)
        products.append((query, grad, scores, dprobs))
    softened = []
    for c in range(GROUP):
        _, _, scores, dprobs = products[c]
        scores = jnp.where(neighbour < count_ref[step * GROUP + c], scores, -jnp.inf)
        powers = jnp.exp(scores - jnp.max(scores, axis=0, keepdims=True))
        probs = powers * (1.0 / jnp.sum(powers, axis=0, keepdims=True))
        row_dot = jnp.sum(probs * dprobs, axis=0, keepdims=True)
        softened.append((probs.astype(BF16), (probs * (dprobs - row_dot)).astype(BF16)))
    for c, (rows, tokens) in enumerate(stretches):
        query, grad, _, _ = products[c]
        weights, dscores = softened[c]
        both_ref[rows, key_cols] = (dot(dscores, query, 1, 0) * factor).astype(BF16)
        both_ref[rows, value_cols] = dot(weights, grad, 1, 0).astype(BF16)
        attended_ref[tokens, :] = join_heads(dot(weights, kv_ref[rows, value_cols], 0, 0)).astype(
            BF16
        )
        grad_query_ref[tokens, :] = (
            join_heads(dot(dscores, kv_ref[rows, key_cols], 0, 0)) * factor
        ).astype(BF16)
    for c, (rows, _) in enumerate(stretches):
        share = dot(both_ref[rows, key_cols], key_weight_ref[...], 1, 1)
        share = share + dot(both_ref[rows, value_cols], value_weight_ref[...], 1, 1)
        share = share.astype(BF16)
        for piece in range(PIECES):
            at = piece * KNB * ROWS
            part = share[at : at + KNB * ROWS].reshape(KNB, ROWS, share.shape[1])
            panels = slice(c * KNB, (c + 1) * KNB)
            share_ref[order_ref[piece] if first else piece, panels] = part
    part = dot(rows_ref[...], both_ref[...], 0, 0)

    @pl.when(step == 0)
    def _():
        total_ref[...] = part if first else begun_ref[...] + part

    @pl.when(step > 0)
    def _():
        total_ref[...] += part

    if not first:

        @pl.when(step == pl.num_programs(0) - 1)
        def _():
            for g in range(4):
                out_ref[g] = total_ref[:, g * DH : (g + 1) * DH].astype(BF16)


def attention(counts, order, panels, w_key, w_value, queries, out_grad, half, begun):
    width, local = w_key.shape
    tokens = HALF * STRETCH
    steps = HALF // GROUP
    half_steps = steps // 2
    first = begun is None
    block = (GROUP * KNB, ROWS, width)
    plain = pl.BlockSpec(block, lambda i, *_: (i, 0, 0))
    low = pl.BlockSpec(block, lambda i, *_: (jnp.minimum(i, half_steps - 1), 0, 0))
    high = pl.BlockSpec(block, lambda i, *_: (jnp.maximum(i - half_steps, 0), 0, 0))
    stacked = lambda begin: pl.BlockSpec((PIECES,) + block, lambda i, *_: (0, begin + i, 0, 0))
    shares = jax.ShapeDtypeStruct((PIECES, CH_DEV * KNB, ROWS, width), BF16)
    token_in = pl.BlockSpec((GROUP * STRETCH, local), lambda i, *_: (i + half * steps, 0))
    token_out = pl.BlockSpec((GROUP * STRETCH, local), lambda i, *_: (i, 0))
    token_shape = jax.ShapeDtypeStruct((tokens, local), BF16)
    whole = lambda shape: pl.BlockSpec(shape, lambda i, *_: (0,) * len(shape))
    total = (width, 2 * local)
    scratch = [
        pltpu.VMEM((GROUP * SPAN, width), BF16),
        pltpu.VMEM((GROUP * SPAN, 2 * local), BF16),
        pltpu.VMEM((GROUP * SPAN, 2 * local), BF16),
    ]
    if first:
        in_specs = [plain, plain, plain, low, high] * 2
        out = jax.ShapeDtypeStruct(total, F32)
        aliases = {}
    else:
        in_specs = [stacked(0), whole(total), pl.BlockSpec(memory_space=pl.ANY)]
        panels = (panels,) + begun
        out = jax.ShapeDtypeStruct((4, width, DH), BF16)
        scratch = scratch + [pltpu.VMEM(total, F32)]
        aliases = {4: 2}
    return pl.pallas_call(
        functools.partial(attention_kernel, first),
        grid_spec=pltpu.PrefetchScalarGridSpec(
            num_scalar_prefetch=2,
            grid=(steps,),
            in_specs=in_specs + [whole(w_key.shape), whole(w_key.shape), token_in, token_in],
            out_specs=[token_out, token_out, stacked(half * steps), whole(out.shape)],
            scratch_shapes=scratch,
        ),
        out_shape=[token_shape, token_shape, shares, out],
        input_output_aliases=aliases,
        compiler_params=pltpu.CompilerParams(vmem_limit_bytes=56 * 2**20),
        cost_estimate=pl.CostEstimate(
            flops=8 * 2**30, bytes_accessed=16 * 2**20, transcendentals=2**18
        ),
        name="attention",
    )(counts, order, *panels, w_key, w_value, queries, out_grad)


def collect_kernel(slot_ref, filled_ref, arrived_ref, out_ref):
    out_ref[...] = jnp.zeros_like(out_ref)

    def one(q, carry):
        @pl.when(filled_ref[q] != 0)
        def _():
            out_ref[slot_ref[q]] += arrived_ref[q].astype(F32)

        return carry

    lax.fori_loop(0, slot_ref.shape[0], one, 0)


def collect(slots, filled, arrived, pool_count):
    count, rows, width = arrived.shape
    return pl.pallas_call(
        collect_kernel,
        grid_spec=pltpu.PrefetchScalarGridSpec(
            num_scalar_prefetch=2,
            grid=(1,),
            in_specs=[pl.BlockSpec((count, rows, width), lambda i, *_: (0, 0, 0))],
            out_specs=pl.BlockSpec((pool_count, rows, width), lambda i, *_: (0, 0, 0)),
        ),
        out_shape=jax.ShapeDtypeStruct((pool_count, rows, width), F32),
        compiler_params=pltpu.CompilerParams(vmem_limit_bytes=16 * 2**20),
        name="collect",
    )(slots, filled, arrived)


def spread_kernel(place_ref, *refs):
    pieces, (key_ref, value_ref, held_ref) = refs[:4], refs[4:]
    for k in range(4):
        held_ref[lax.rem(place_ref[0] - k + 4, 4)] = pieces[k][...].astype(F32)
    key_ref[:, :DH], key_ref[:, DH:] = held_ref[0], held_ref[1]
    value_ref[:, :DH], value_ref[:, DH:] = held_ref[2], held_ref[3]


def spread_columns(column, place):
    width = column.shape[0]
    pieces = [column] + [lax.ppermute(column, "x", shift(4, k)) for k in (1, 3, 2)]
    pieces = [pieces[0], pieces[1], pieces[3], pieces[2]]
    shape = jax.ShapeDtypeStruct((width, 2 * DH), F32)
    return pl.pallas_call(
        spread_kernel,
        grid_spec=pltpu.PrefetchScalarGridSpec(
            num_scalar_prefetch=1,
            grid=(1,),
            in_specs=[pl.BlockSpec(column.shape, lambda i, *_: (0, 0))] * 4,
            out_specs=[pl.BlockSpec(shape.shape, lambda i, *_: (0, 0))] * 2,
            scratch_shapes=[pltpu.VMEM((4, width, DH), F32)],
        ),
        out_shape=[shape, shape],
        compiler_params=pltpu.CompilerParams(vmem_limit_bytes=16 * 2**20),
        name="spread",
    )(place, *pieces)


def exchange(array):
    return lax.all_to_all(array, ("z", "x"), split_axis=0, concat_axis=0, tiled=True)


def local(queries, pool, w_key, w_value, out_grad, nb_source, nb_slot, nb_count):
    seq_count = lax.axis_size(("z", "x"))
    seq_index = lax.axis_index(("z", "x"))
    requests = CH_DEV * KNB
    capacity = max(2, 2 * requests // seq_count)
    slot_span = seq_count * capacity
    source_table = nb_source.reshape(seq_count, requests)
    slot_table = nb_slot.reshape(seq_count, requests)
    order_ids = jnp.arange(requests)
    matches = source_table[:, :, None] == source_table[:, None, :]
    before = order_ids[None, :] < order_ids[:, None]
    ranks = jnp.sum(jnp.logical_and(matches, before[None, :, :]), axis=2)
    places = jnp.arange(capacity)
    chosen = jnp.logical_and(
        (source_table == seq_index)[:, :, None], ranks[:, :, None] == places[None, None, :]
    )
    picked_slot = jnp.sum(jnp.where(chosen, slot_table[:, :, None], 0), axis=1).reshape(slot_span)
    filled = jnp.any(chosen, axis=1).reshape(slot_span).astype(jnp.int32)
    own_sources = lax.dynamic_index_in_dim(source_table, seq_index, 0, keepdims=False)
    own_ranks = lax.dynamic_index_in_dim(ranks, seq_index, 0, keepdims=False)
    positions = own_sources * capacity + own_ranks
    back = jnp.sum(
        jnp.where(positions[None, :] == jnp.arange(slot_span)[:, None], order_ids[None, :], 0), axis=1
    )
    counts = lax.dynamic_slice_in_dim(nb_count, seq_index * CH_DEV, CH_DEV)
    take = lambda array, index: jnp.take(array, index, axis=0, mode="clip")

    incoming = exchange(take(pool, picked_slot))
    y, core = lax.axis_index("y"), lax.axis_index("core")
    order = jnp.stack(
        [(y + dy) % 4 * 2 + (core + other) % 2 for other in (0, 1) for dy in (0, 1, 3, 2)]
    ).astype(jnp.int32)
    place = lax.axis_index("x").astype(jnp.int32).reshape(1)
    positions, back, counts, order, filled, place = lax.optimization_barrier(
        (positions, back, counts, order, filled, place)
    )
    panels = HALF * KNB
    pieces = gather_pieces(take(incoming, positions[:panels]))
    gathered = lax.all_gather(take(incoming, positions[panels:]), ("y", "core"), axis=0)
    weights = (w_key, w_value, queries, out_grad)
    attended_0, grad_queries_0, shares, begun = attention(
        counts[:HALF], order, pieces, *weights, 0, None
    )
    attended_1, grad_queries_1, shares, parts = attention(
        counts[HALF:], order, gathered, *weights, 1, (begun, shares)
    )
    summed = lax.psum_scatter(shares, ("y", "core"), scatter_dimension=0)
    column = reduce_weight_grads(parts)
    returning = take(summed, back)
    returning, column = lax.optimization_barrier((returning, column))
    arrived = exchange(returning)
    grad_w_key, grad_w_value = spread_columns(column, place)
    grad_pool = collect(picked_slot, filled, arrived, pool.shape[0])
    return (
        jnp.concatenate([attended_0, attended_1]),
        jnp.concatenate([grad_queries_0, grad_queries_1]),
        grad_pool,
        grad_w_key,
        grad_w_value,
    )


def solution(mesh):
    grid = Mesh(mesh.devices.reshape(8, 4, 4, 2), ("z", "x", "y", "core"))
    seq, head = ("z", "x"), ("y", "core")
    return jax.shard_map(
        local,
        mesh=grid,
        in_specs=(
            P(seq, head),
            P(seq, head, None),
            P(None, head),
            P(None, head),
            P(seq, head),
            P(),
            P(),
            P(),
        ),
        out_specs=(
            P(seq, head),
            P(seq, head),
            P(seq, head, None),
            P(None, head),
            P(None, head),
        ),
        check_vma=False,
    )
```

```python
import functools
import math

import jax
import jax.numpy as jnp
from jax import lax
from jax.experimental import pallas as pl
from jax.experimental.pallas import tpu as pltpu
from jax.sharding import Mesh
from jax.sharding import PartitionSpec as P

DH = 128
STRETCH = 64
KNB = 2
CH_DEV = 16
ROWS = 16
PIECES = 8
SPAN = KNB * ROWS * PIECES
HALF = 8
GROUP = 4
F32 = jnp.float32
BF16 = jnp.bfloat16

UP = [(i, (i + 1) % 4) for i in range(4)]
DOWN = [((i + 1) % 4, i) for i in range(4)]
SWAP = [(0, 1), (1, 0)]


def dot(a, b, ca, cb):
    return lax.dot_general(a, b, (((ca,), (cb,)), ((), ())), preferred_element_type=F32)


def shift(size, k):
    return [(i, (i + k) % size) for i in range(size)]


def gather_pieces(own):
    half = own.shape[0] // 2
    below = lax.ppermute(own, "y", UP)
    above = lax.ppermute(own, "y", DOWN)
    far_low = lax.ppermute(below[:half], "y", UP)
    far_high = lax.ppermute(above[half:], "y", DOWN)
    mine = [own, above, below, far_low, far_high]
    return mine + [lax.ppermute(piece, "core", SWAP) for piece in mine]


def plus(*terms):
    total = terms[0].astype(F32)
    for term in terms[1:]:
        total = total + term.astype(F32)
    return total


def scatter_and_reduce(mine, other, parts):
    half = mine.shape[1] // 2
    swapped = lax.ppermute(other, "core", SWAP)
    far = plus(mine[3], swapped[3]).astype(BF16)
    far, parts = lax.optimization_barrier((far, parts))
    got_low = lax.ppermute(far[:half], "y", UP)
    got_high = lax.ppermute(far[half:], "y", DOWN)
    by_x = lax.all_to_all(parts, "x", split_axis=0, concat_axis=0, tiled=True)
    part = plus(*[by_x[k] for k in range(4)]).astype(BF16).reshape(8, -1, DH)
    up_low = plus(mine[1, :half], swapped[1, :half], got_low).astype(BF16)
    up_high = plus(mine[1, half:], swapped[1, half:]).astype(BF16)
    down_low = plus(mine[2, :half], swapped[2, :half]).astype(BF16)
    down_high = plus(mine[2, half:], swapped[2, half:], got_high).astype(BF16)
    up = jnp.concatenate([up_low, up_high])
    down = jnp.concatenate([down_low, down_high])
    up, down, part = lax.optimization_barrier((up, down, part))
    from_below = lax.ppermute(up, "y", UP)
    from_above = lax.ppermute(down, "y", DOWN)
    by_z = lax.all_to_all(part, "z", split_axis=0, concat_axis=0, tiled=True)
    total = plus(*[by_z[k] for k in range(8)]).astype(BF16)
    summed = plus(mine[0], swapped[0], from_below, from_above).astype(BF16)
    return summed, total


def fill_from_pieces(step, refs, rows_ref):
    half_steps = HALF // GROUP // 2
    for core in range(2):
        own, above, below, far_low, far_high = refs[core * 5 : core * 5 + 5]

        def put(place, ref):
            for c in range(GROUP):
                at = c * SPAN + (core * 4 + place) * KNB * ROWS
                rows_ref[at : at + KNB * ROWS, :] = ref[c * KNB : (c + 1) * KNB].reshape(
                    KNB * ROWS, ref.shape[2]
                )

        put(0, own)
        put(1, above)
        put(2, below)

        @pl.when(step < half_steps)
        def _():
            put(3, far_low)

        @pl.when(step >= half_steps)
        def _():
            put(3, far_high)


def fill_from_gathered(order_ref, gathered_ref, rows_ref):
    for piece in range(PIECES):
        source = order_ref[piece]
        for c in range(GROUP):
            at = c * SPAN + piece * KNB * ROWS
            rows_ref[at : at + KNB * ROWS, :] = gathered_ref[
                source, c * KNB : (c + 1) * KNB
            ].reshape(KNB * ROWS, gathered_ref.shape[3])


def attention_kernel(first, count_ref, order_ref, *refs):
    step = pl.program_id(0)
    if first:
        pieces, refs = refs[:10], refs[10:]
    else:
        gathered_ref, begun_ref, refs = refs[0], refs[1], refs[2:]
    key_weight_ref, value_weight_ref, query_ref, grad_ref, attended_ref, grad_query_ref = refs[:6]
    refs = refs[6:]
    if first:
        share_ref, out_ref, rows_ref, kv_ref, both_ref = refs
        total_ref = out_ref
        fill_from_pieces(step, pieces, rows_ref)
    else:
        mine_ref, other_ref, out_ref, rows_ref, kv_ref, both_ref, total_ref = refs
        fill_from_gathered(order_ref, gathered_ref, rows_ref)
    local = key_weight_ref.shape[1]
    factor = 1.0 / math.sqrt(DH)
    key_cols, value_cols = slice(0, local), slice(local, 2 * local)
    head_of = lax.broadcasted_iota(jnp.int32, (STRETCH, local), 1) < DH
    neighbour = (lax.broadcasted_iota(jnp.int32, (SPAN, 1), 0) // ROWS) % KNB

    def spread_heads(x):
        zero = jnp.zeros_like(x)
        return jnp.concatenate([jnp.where(head_of, x, zero), jnp.where(head_of, zero, x)], axis=0)

    def join_heads(x):
        return jnp.where(head_of, x[:STRETCH], x[STRETCH:])

    stretches = [
        (slice(c * SPAN, (c + 1) * SPAN), slice(c * STRETCH, (c + 1) * STRETCH))
        for c in range(GROUP)
    ]
    for rows, _ in stretches:
        panel = rows_ref[rows, :]
        kv_ref[rows, key_cols] = dot(panel, key_weight_ref[...], 1, 0).astype(BF16)
        kv_ref[rows, value_cols] = dot(panel, value_weight_ref[...], 1, 0).astype(BF16)
    products = []
    for rows, tokens in stretches:
        query, grad = spread_heads(query_ref[tokens, :]), spread_heads(grad_ref[tokens, :])
        scores = dot(kv_ref[rows, key_cols], query, 1, 1) * factor
        dprobs = dot(kv_ref[rows, value_cols], grad, 1, 1)
        products.append((query, grad, scores, dprobs))
    softened = []
    for c in range(GROUP):
        _, _, scores, dprobs = products[c]
        scores = jnp.where(neighbour < count_ref[step * GROUP + c], scores, -jnp.inf)
        powers = jnp.exp(scores - jnp.max(scores, axis=0, keepdims=True))
        probs = powers * (1.0 / jnp.sum(powers, axis=0, keepdims=True))
        row_dot = jnp.sum(probs * dprobs, axis=0, keepdims=True)
        softened.append((probs.astype(BF16), (probs * (dprobs - row_dot)).astype(BF16)))
    for c, (rows, tokens) in enumerate(stretches):
        query, grad, _, _ = products[c]
        weights, dscores = softened[c]
        both_ref[rows, key_cols] = (dot(dscores, query, 1, 0) * factor).astype(BF16)
        both_ref[rows, value_cols] = dot(weights, grad, 1, 0).astype(BF16)
        attended_ref[tokens, :] = join_heads(dot(weights, kv_ref[rows, value_cols], 0, 0)).astype(
            BF16
        )
        grad_query_ref[tokens, :] = (
            join_heads(dot(dscores, kv_ref[rows, key_cols], 0, 0)) * factor
        ).astype(BF16)
    for c, (rows, _) in enumerate(stretches):
        share = dot(both_ref[rows, key_cols], key_weight_ref[...], 1, 1)
        share = share + dot(both_ref[rows, value_cols], value_weight_ref[...], 1, 1)
        share = share.astype(BF16)
        for piece in range(PIECES):
            at = piece * KNB * ROWS
            part = share[at : at + KNB * ROWS].reshape(KNB, ROWS, share.shape[1])
            panels = slice(c * KNB, (c + 1) * KNB)
            if first:
                share_ref[order_ref[piece], panels] = part
            elif piece < 4:
                mine_ref[piece, panels] = part
            else:
                other_ref[piece - 4, panels] = part
    part = dot(rows_ref[...], both_ref[...], 0, 0)

    @pl.when(step == 0)
    def _():
        total_ref[...] = part if first else begun_ref[...] + part

    @pl.when(step > 0)
    def _():
        total_ref[...] += part

    if not first:

        @pl.when(step == pl.num_programs(0) - 1)
        def _():
            for g in range(4):
                out_ref[g] = total_ref[:, g * DH : (g + 1) * DH].astype(BF16)


def attention(counts, order, panels, w_key, w_value, queries, out_grad, half, begun):
    width, local = w_key.shape
    tokens = HALF * STRETCH
    steps = HALF // GROUP
    half_steps = steps // 2
    first = begun is None
    block = (GROUP * KNB, ROWS, width)
    plain = pl.BlockSpec(block, lambda i, *_: (i, 0, 0))
    low = pl.BlockSpec(block, lambda i, *_: (jnp.minimum(i, half_steps - 1), 0, 0))
    high = pl.BlockSpec(block, lambda i, *_: (jnp.maximum(i - half_steps, 0), 0, 0))
    stacked = lambda n: pl.BlockSpec((n,) + block, lambda i, *_: (0, i, 0, 0))
    stacked_shape = lambda n: jax.ShapeDtypeStruct((n, HALF * KNB, ROWS, width), BF16)
    token_in = pl.BlockSpec((GROUP * STRETCH, local), lambda i, *_: (i + half * steps, 0))
    token_out = pl.BlockSpec((GROUP * STRETCH, local), lambda i, *_: (i, 0))
    token_shape = jax.ShapeDtypeStruct((tokens, local), BF16)
    whole = lambda shape: pl.BlockSpec(shape, lambda i, *_: (0,) * len(shape))
    total = (width, 2 * local)
    scratch = [
        pltpu.VMEM((GROUP * SPAN, width), BF16),
        pltpu.VMEM((GROUP * SPAN, 2 * local), BF16),
        pltpu.VMEM((GROUP * SPAN, 2 * local), BF16),
    ]
    if first:
        in_specs = [plain, plain, plain, low, high] * 2
        share_specs, share_shapes = [stacked(PIECES)], [stacked_shape(PIECES)]
        out = jax.ShapeDtypeStruct(total, F32)
    else:
        in_specs = [stacked(PIECES), whole(total)]
        panels = [panels, begun]
        share_specs, share_shapes = [stacked(4)] * 2, [stacked_shape(4)] * 2
        out = jax.ShapeDtypeStruct((4, width, DH), BF16)
        scratch = scratch + [pltpu.VMEM(total, F32)]
    return pl.pallas_call(
        functools.partial(attention_kernel, first),
        grid_spec=pltpu.PrefetchScalarGridSpec(
            num_scalar_prefetch=2,
            grid=(steps,),
            in_specs=in_specs + [whole(w_key.shape), whole(w_key.shape), token_in, token_in],
            out_specs=[token_out, token_out] + share_specs + [whole(out.shape)],
            scratch_shapes=scratch,
        ),
        out_shape=[token_shape, token_shape] + share_shapes + [out],
        compiler_params=pltpu.CompilerParams(vmem_limit_bytes=56 * 2**20),
        cost_estimate=pl.CostEstimate(
            flops=8 * 2**30, bytes_accessed=16 * 2**20, transcendentals=2**18
        ),
        name="attention",
    )(counts, order, *panels, w_key, w_value, queries, out_grad)


def collect_kernel(slot_ref, filled_ref, arrived_ref, out_ref):
    out_ref[...] = jnp.zeros_like(out_ref)

    def one(q, carry):
        @pl.when(filled_ref[q] != 0)
        def _():
            out_ref[slot_ref[q]] += arrived_ref[q].astype(F32)

        return carry

    lax.fori_loop(0, slot_ref.shape[0], one, 0)


def collect(slots, filled, arrived, pool_count):
    count, rows, width = arrived.shape
    return pl.pallas_call(
        collect_kernel,
        grid_spec=pltpu.PrefetchScalarGridSpec(
            num_scalar_prefetch=2,
            grid=(1,),
            in_specs=[pl.BlockSpec((count, rows, width), lambda i, *_: (0, 0, 0))],
            out_specs=pl.BlockSpec((pool_count, rows, width), lambda i, *_: (0, 0, 0)),
        ),
        out_shape=jax.ShapeDtypeStruct((pool_count, rows, width), F32),
        compiler_params=pltpu.CompilerParams(vmem_limit_bytes=16 * 2**20),
        name="collect",
    )(slots, filled, arrived)


def spread_kernel(place_ref, *refs):
    pieces, (key_ref, value_ref, held_ref) = refs[:4], refs[4:]
    x, z = place_ref[0], place_ref[1]
    rows = key_ref.shape[0] // 8
    for k in range(4):
        group = lax.rem(x - k + 4, 4)
        for j in range(8):
            at = pl.multiple_of(jnp.bitwise_xor(z, j) * rows, 16)
            part = pieces[k][j * rows : (j + 1) * rows, :]
            held_ref[group, pl.ds(at, rows), :] = part.astype(F32)
    key_ref[:, :DH], key_ref[:, DH:] = held_ref[0], held_ref[1]
    value_ref[:, :DH], value_ref[:, DH:] = held_ref[2], held_ref[3]


def spread_columns(block, place):
    column = block
    for bit in (1, 2, 4):
        swap = [(i, i ^ bit) for i in range(8)]
        column = jnp.concatenate([column, lax.ppermute(column, "z", swap)])
    width = column.shape[0]
    pieces = [column] + [lax.ppermute(column, "x", shift(4, k)) for k in (1, 3, 2)]
    pieces = [pieces[0], pieces[1], pieces[3], pieces[2]]
    shape = jax.ShapeDtypeStruct((width, 2 * DH), F32)
    return pl.pallas_call(
        spread_kernel,
        grid_spec=pltpu.PrefetchScalarGridSpec(
            num_scalar_prefetch=1,
            grid=(1,),
            in_specs=[pl.BlockSpec(column.shape, lambda i, *_: (0, 0))] * 4,
            out_specs=[pl.BlockSpec(shape.shape, lambda i, *_: (0, 0))] * 2,
            scratch_shapes=[pltpu.VMEM((4, width, DH), F32)],
        ),
        out_shape=[shape, shape],
        compiler_params=pltpu.CompilerParams(vmem_limit_bytes=16 * 2**20),
        name="spread",
    )(place, *pieces)


def exchange(array):
    return lax.all_to_all(array, ("z", "x"), split_axis=0, concat_axis=0, tiled=True)


def local(queries, pool, w_key, w_value, out_grad, nb_source, nb_slot, nb_count):
    seq_count = lax.axis_size(("z", "x"))
    seq_index = lax.axis_index(("z", "x"))
    requests = CH_DEV * KNB
    capacity = max(2, 2 * requests // seq_count)
    slot_span = seq_count * capacity
    source_table = nb_source.reshape(seq_count, requests)
    slot_table = nb_slot.reshape(seq_count, requests)
    order_ids = jnp.arange(requests)
    matches = source_table[:, :, None] == source_table[:, None, :]
    before = order_ids[None, :] < order_ids[:, None]
    ranks = jnp.sum(jnp.logical_and(matches, before[None, :, :]), axis=2)
    places = jnp.arange(capacity)
    chosen = jnp.logical_and(
        (source_table == seq_index)[:, :, None], ranks[:, :, None] == places[None, None, :]
    )
    picked_slot = jnp.sum(jnp.where(chosen, slot_table[:, :, None], 0), axis=1).reshape(slot_span)
    filled = jnp.any(chosen, axis=1).reshape(slot_span).astype(jnp.int32)
    own_sources = lax.dynamic_index_in_dim(source_table, seq_index, 0, keepdims=False)
    own_ranks = lax.dynamic_index_in_dim(ranks, seq_index, 0, keepdims=False)
    positions = own_sources * capacity + own_ranks
    back = jnp.sum(
        jnp.where(positions[None, :] == jnp.arange(slot_span)[:, None], order_ids[None, :], 0), axis=1
    )
    counts = lax.dynamic_slice_in_dim(nb_count, seq_index * CH_DEV, CH_DEV)
    take = lambda array, index: jnp.take(array, index, axis=0, mode="clip")

    incoming = exchange(take(pool, picked_slot))
    y, core = lax.axis_index("y"), lax.axis_index("core")
    order = jnp.stack(
        [(y + dy) % 4 * 2 + (core + other) % 2 for other in (0, 1) for dy in (0, 1, 3, 2)]
    ).astype(jnp.int32)
    place = jnp.stack([lax.axis_index("x"), lax.axis_index("z")]).astype(jnp.int32)
    positions, back, counts, order, filled, place = lax.optimization_barrier(
        (positions, back, counts, order, filled, place)
    )
    panels = HALF * KNB
    pieces = gather_pieces(take(incoming, positions[:panels]))
    gathered = lax.all_gather(take(incoming, positions[panels:]), ("y", "core"), axis=0)
    weights = (w_key, w_value, queries, out_grad)
    attended_0, grad_queries_0, share, begun = attention(
        counts[:HALF], order, pieces, *weights, 0, None
    )
    summed_0 = lax.psum_scatter(share, ("y", "core"), scatter_dimension=0)
    attended_1, grad_queries_1, mine, other, parts = attention(
        counts[HALF:], order, gathered, *weights, 1, begun
    )
    summed_1, total = scatter_and_reduce(mine, other, parts)
    returning = take(jnp.concatenate([summed_0, summed_1]), back)
    returning, total = lax.optimization_barrier((returning, total))
    arrived = exchange(returning)
    grad_w_key, grad_w_value = spread_columns(total, place)
    grad_pool = collect(picked_slot, filled, arrived, pool.shape[0])
    return (
        jnp.concatenate([attended_0, attended_1]),
        jnp.concatenate([grad_queries_0, grad_queries_1]),
        grad_pool,
        grad_w_key,
        grad_w_value,
    )


def solution(mesh):
    grid = Mesh(mesh.devices.reshape(8, 4, 4, 2), ("z", "x", "y", "core"))
    seq, head = ("z", "x"), ("y", "core")
    return jax.shard_map(
        local,
        mesh=grid,
        in_specs=(
            P(seq, head),
            P(seq, head, None),
            P(None, head),
            P(None, head),
            P(seq, head),
            P(),
            P(),
            P(),
        ),
        out_specs=(
            P(seq, head),
            P(seq, head),
            P(seq, head, None),
            P(None, head),
            P(None, head),
        ),
        check_vma=False,
    )
```

```python
import functools
import math

import jax
import jax.numpy as jnp
from jax import lax
from jax.experimental import pallas as pl
from jax.experimental.pallas import tpu as pltpu
from jax.sharding import Mesh
from jax.sharding import PartitionSpec as P

DH = 128
STRETCH = 64
KNB = 2
CH_DEV = 16
ROWS = 16
PIECES = 8
SPAN = KNB * ROWS * PIECES
PARTS = ((0, 6, 3), (6, 10, 2))
F32 = jnp.float32
BF16 = jnp.bfloat16

UP = [(i, (i + 1) % 4) for i in range(4)]
DOWN = [((i + 1) % 4, i) for i in range(4)]
SWAP = [(0, 1), (1, 0)]


def dot(a, b, ca, cb):
    return lax.dot_general(a, b, (((ca,), (cb,)), ((), ())), preferred_element_type=F32)


def shift(size, k):
    return [(i, (i + k) % size) for i in range(size)]


def gather_pieces(own):
    half = own.shape[0] // 2
    below = lax.ppermute(own, "y", UP)
    above = lax.ppermute(own, "y", DOWN)
    far_low = lax.ppermute(below[:half], "y", UP)
    far_high = lax.ppermute(above[half:], "y", DOWN)
    mine = [own, above, below, far_low, far_high]
    return mine + [lax.ppermute(piece, "core", SWAP) for piece in mine]


def plus(*terms):
    total = terms[0].astype(F32)
    for term in terms[1:]:
        total = total + term.astype(F32)
    return total


def reduce_weight_grads(parts):
    by_x = lax.all_to_all(parts, "x", split_axis=0, concat_axis=0, tiled=True)
    part = plus(*[by_x[k] for k in range(4)]).astype(BF16).reshape(8, -1, DH)
    by_z = lax.all_to_all(part, "z", split_axis=0, concat_axis=0, tiled=True)
    total = plus(*[by_z[k] for k in range(8)]).astype(BF16)
    column = jnp.broadcast_to(total[None], part.shape)
    column = lax.all_to_all(column, "z", split_axis=0, concat_axis=0, tiled=True)
    return column.reshape(-1, DH)


def fill_from_pieces(step, group, half_steps, refs, rows_ref):
    for core in range(2):
        own, above, below, far_low, far_high = refs[core * 5 : core * 5 + 5]

        def put(place, ref):
            for c in range(group):
                at = c * SPAN + (core * 4 + place) * KNB * ROWS
                rows_ref[at : at + KNB * ROWS, :] = ref[c * KNB : (c + 1) * KNB].reshape(
                    KNB * ROWS, ref.shape[2]
                )

        put(0, own)
        put(1, above)
        put(2, below)

        @pl.when(step < half_steps)
        def _():
            put(3, far_low)

        @pl.when(step >= half_steps)
        def _():
            put(3, far_high)


def fill_from_gathered(group, gathered_ref, rows_ref):
    for piece in range(PIECES):
        for c in range(group):
            at = c * SPAN + piece * KNB * ROWS
            rows_ref[at : at + KNB * ROWS, :] = gathered_ref[
                piece, c * KNB : (c + 1) * KNB
            ].reshape(KNB * ROWS, gathered_ref.shape[3])


def attention_kernel(first, begin, stretch_count, group, count_ref, order_ref, *refs):
    step = pl.program_id(0)
    if first:
        pieces, refs = refs[:10], refs[10:]
    else:
        gathered_ref, begun_ref, _, refs = refs[0], refs[1], refs[2], refs[3:]
    key_weight_ref, value_weight_ref, query_ref, grad_ref, attended_ref, grad_query_ref = refs[:6]
    refs = refs[6:]
    share_ref, out_ref, rows_ref, kv_ref, both_ref, total_ref = refs
    if first:
        fill_from_pieces(step, group, stretch_count // group // 2, pieces, rows_ref)
    else:
        fill_from_gathered(group, gathered_ref, rows_ref)
    local = key_weight_ref.shape[1]
    factor = 1.0 / math.sqrt(DH)
    key_cols, value_cols = slice(0, local), slice(local, 2 * local)
    head_of = lax.broadcasted_iota(jnp.int32, (STRETCH, local), 1) < DH
    neighbour = (lax.broadcasted_iota(jnp.int32, (SPAN, 1), 0) // ROWS) % KNB

    def spread_heads(x):
        zero = jnp.zeros_like(x)
        return jnp.concatenate([jnp.where(head_of, x, zero), jnp.where(head_of, zero, x)], axis=0)

    def join_heads(x):
        return jnp.where(head_of, x[:STRETCH], x[STRETCH:])

    stretches = [
        (slice(c * SPAN, (c + 1) * SPAN), slice(c * STRETCH, (c + 1) * STRETCH))
        for c in range(group)
    ]
    for rows, _ in stretches:
        panel = rows_ref[rows, :]
        kv_ref[rows, key_cols] = dot(panel, key_weight_ref[...], 1, 0).astype(BF16)
        kv_ref[rows, value_cols] = dot(panel, value_weight_ref[...], 1, 0).astype(BF16)
    products = []
    for rows, tokens in stretches:
        query, grad = spread_heads(query_ref[tokens, :]), spread_heads(grad_ref[tokens, :])
        scores = dot(kv_ref[rows, key_cols], query, 1, 1) * factor
        dprobs = dot(kv_ref[rows, value_cols], grad, 1, 1)
        products.append((query, grad, scores, dprobs))
    softened = []
    for c in range(group):
        _, _, scores, dprobs = products[c]
        scores = jnp.where(neighbour < count_ref[begin + step * group + c], scores, -jnp.inf)
        powers = jnp.exp(scores - jnp.max(scores, axis=0, keepdims=True))
        probs = powers * (1.0 / jnp.sum(powers, axis=0, keepdims=True))
        row_dot = jnp.sum(probs * dprobs, axis=0, keepdims=True)
        softened.append((probs.astype(BF16), (probs * (dprobs - row_dot)).astype(BF16)))
    for c, (rows, tokens) in enumerate(stretches):
        query, grad, _, _ = products[c]
        weights, dscores = softened[c]
        both_ref[rows, key_cols] = (dot(dscores, query, 1, 0) * factor).astype(BF16)
        both_ref[rows, value_cols] = dot(weights, grad, 1, 0).astype(BF16)
        attended_ref[tokens, :] = join_heads(dot(weights, kv_ref[rows, value_cols], 0, 0)).astype(
            BF16
        )
        grad_query_ref[tokens, :] = (
            join_heads(dot(dscores, kv_ref[rows, key_cols], 0, 0)) * factor
        ).astype(BF16)
    for c, (rows, _) in enumerate(stretches):
        share = dot(both_ref[rows, key_cols], key_weight_ref[...], 1, 1)
        share = share + dot(both_ref[rows, value_cols], value_weight_ref[...], 1, 1)
        share = share.astype(BF16)
        for piece in range(PIECES):
            at = piece * KNB * ROWS
            part = share[at : at + KNB * ROWS].reshape(KNB, ROWS, share.shape[1])
            panels = slice(c * KNB, (c + 1) * KNB)
            share_ref[order_ref[piece] if first else piece, panels] = part
    part = dot(rows_ref[...], both_ref[...], 0, 0)

    @pl.when(step == 0)
    def _():
        total_ref[...] = part if first else begun_ref[...].astype(F32) + part

    @pl.when(step > 0)
    def _():
        total_ref[...] += part

    @pl.when(step == pl.num_programs(0) - 1)
    def _():
        if first:
            out_ref[...] = total_ref[...].astype(BF16)
        else:
            for g in range(4):
                out_ref[g] = total_ref[:, g * DH : (g + 1) * DH].astype(BF16)


def attention(counts, order, panels, w_key, w_value, queries, out_grad, part, begun):
    width, local = w_key.shape
    begin, stretch_count, group = part
    tokens = stretch_count * STRETCH
    steps, skip = stretch_count // group, begin // group
    half_steps = steps // 2
    first = begun is None
    block = (group * KNB, ROWS, width)
    plain = pl.BlockSpec(block, lambda i, *_: (i, 0, 0))
    low = pl.BlockSpec(block, lambda i, *_: (jnp.minimum(i, half_steps - 1), 0, 0))
    high = pl.BlockSpec(block, lambda i, *_: (jnp.maximum(i - half_steps, 0), 0, 0))
    stacked = lambda skip: pl.BlockSpec((PIECES,) + block, lambda i, *_: (0, skip + i, 0, 0))
    shares = jax.ShapeDtypeStruct((PIECES, CH_DEV * KNB, ROWS, width), BF16)
    token_in = pl.BlockSpec((group * STRETCH, local), lambda i, *_: (i + skip, 0))
    token_out = pl.BlockSpec((group * STRETCH, local), lambda i, *_: (i, 0))
    token_shape = jax.ShapeDtypeStruct((tokens, local), BF16)
    whole = lambda shape: pl.BlockSpec(shape, lambda i, *_: (0,) * len(shape))
    total = (width, 2 * local)
    scratch = [
        pltpu.VMEM((group * SPAN, width), BF16),
        pltpu.VMEM((group * SPAN, 2 * local), BF16),
        pltpu.VMEM((group * SPAN, 2 * local), BF16),
        pltpu.VMEM(total, F32),
    ]
    if first:
        in_specs = [plain, plain, plain, low, high] * 2
        out = jax.ShapeDtypeStruct(total, BF16)
        aliases = {}
    else:
        in_specs = [stacked(0), whole(total), pl.BlockSpec(memory_space=pl.ANY)]
        panels = (panels,) + begun
        out = jax.ShapeDtypeStruct((4, width, DH), BF16)
        aliases = {4: 2}
    return pl.pallas_call(
        functools.partial(attention_kernel, first, begin, stretch_count, group),
        grid_spec=pltpu.PrefetchScalarGridSpec(
            num_scalar_prefetch=2,
            grid=(steps,),
            in_specs=in_specs + [whole(w_key.shape), whole(w_key.shape), token_in, token_in],
            out_specs=[token_out, token_out, stacked(skip), whole(out.shape)],
            scratch_shapes=scratch,
        ),
        out_shape=[token_shape, token_shape, shares, out],
        input_output_aliases=aliases,
        compiler_params=pltpu.CompilerParams(vmem_limit_bytes=56 * 2**20),
        cost_estimate=pl.CostEstimate(
            flops=8 * 2**30, bytes_accessed=16 * 2**20, transcendentals=2**18
        ),
        name="attention",
    )(counts, order, *panels, w_key, w_value, queries, out_grad)


def collect_kernel(slot_ref, filled_ref, arrived_ref, out_ref):
    out_ref[...] = jnp.zeros_like(out_ref)

    def one(q, carry):
        @pl.when(filled_ref[q] != 0)
        def _():
            out_ref[slot_ref[q]] += arrived_ref[q].astype(F32)

        return carry

    lax.fori_loop(0, slot_ref.shape[0], one, 0)


def collect(slots, filled, arrived, pool_count):
    count, rows, width = arrived.shape
    return pl.pallas_call(
        collect_kernel,
        grid_spec=pltpu.PrefetchScalarGridSpec(
            num_scalar_prefetch=2,
            grid=(1,),
            in_specs=[pl.BlockSpec((count, rows, width), lambda i, *_: (0, 0, 0))],
            out_specs=pl.BlockSpec((pool_count, rows, width), lambda i, *_: (0, 0, 0)),
        ),
        out_shape=jax.ShapeDtypeStruct((pool_count, rows, width), F32),
        compiler_params=pltpu.CompilerParams(vmem_limit_bytes=16 * 2**20),
        name="collect",
    )(slots, filled, arrived)


def spread_kernel(place_ref, *refs):
    pieces, (key_ref, value_ref, held_ref) = refs[:4], refs[4:]
    for k in range(4):
        held_ref[lax.rem(place_ref[0] - k + 4, 4)] = pieces[k][...].astype(F32)
    key_ref[:, :DH], key_ref[:, DH:] = held_ref[0], held_ref[1]
    value_ref[:, :DH], value_ref[:, DH:] = held_ref[2], held_ref[3]


def spread_columns(column, place):
    width = column.shape[0]
    pieces = [column] + [lax.ppermute(column, "x", shift(4, k)) for k in (1, 3, 2)]
    pieces = [pieces[0], pieces[1], pieces[3], pieces[2]]
    shape = jax.ShapeDtypeStruct((width, 2 * DH), F32)
    return pl.pallas_call(
        spread_kernel,
        grid_spec=pltpu.PrefetchScalarGridSpec(
            num_scalar_prefetch=1,
            grid=(1,),
            in_specs=[pl.BlockSpec(column.shape, lambda i, *_: (0, 0))] * 4,
            out_specs=[pl.BlockSpec(shape.shape, lambda i, *_: (0, 0))] * 2,
            scratch_shapes=[pltpu.VMEM((4, width, DH), F32)],
        ),
        out_shape=[shape, shape],
        compiler_params=pltpu.CompilerParams(vmem_limit_bytes=16 * 2**20),
        name="spread",
    )(place, *pieces)


def exchange(array):
    return lax.all_to_all(array, ("z", "x"), split_axis=0, concat_axis=0, tiled=True)


def local(queries, pool, w_key, w_value, out_grad, nb_source, nb_slot, nb_count):
    seq_count = lax.axis_size(("z", "x"))
    seq_index = lax.axis_index(("z", "x"))
    requests = CH_DEV * KNB
    capacity = max(2, 2 * requests // seq_count)
    slot_span = seq_count * capacity
    pool_count = pool.shape[0]
    packed = (nb_source * pool_count + nb_slot).reshape(seq_count, requests)
    source_table, slot_table = packed // pool_count, packed % pool_count
    order_ids = jnp.arange(requests)
    matches = source_table[:, :, None] == source_table[:, None, :]
    before = order_ids[None, :] < order_ids[:, None]
    ranks = jnp.sum(jnp.logical_and(matches, before[None, :, :]), axis=2)
    places = jnp.arange(capacity)
    chosen = jnp.logical_and(
        (source_table == seq_index)[:, :, None], ranks[:, :, None] == places[None, None, :]
    )
    picked_slot = jnp.sum(jnp.where(chosen, slot_table[:, :, None], 0), axis=1).reshape(slot_span)
    filled = jnp.any(chosen, axis=1).reshape(slot_span).astype(jnp.int32)
    own_sources = lax.dynamic_index_in_dim(source_table, seq_index, 0, keepdims=False)
    own_ranks = lax.dynamic_index_in_dim(ranks, seq_index, 0, keepdims=False)
    positions = own_sources * capacity + own_ranks
    back = jnp.sum(
        jnp.where(positions[None, :] == jnp.arange(slot_span)[:, None], order_ids[None, :], 0), axis=1
    )
    counts = lax.dynamic_slice_in_dim(nb_count, seq_index * CH_DEV, CH_DEV)
    take = lambda array, index: jnp.take(array, index, axis=0, mode="clip")

    incoming = exchange(take(pool, picked_slot))
    y, core = lax.axis_index("y"), lax.axis_index("core")
    order = jnp.stack(
        [(y + dy) % 4 * 2 + (core + other) % 2 for other in (0, 1) for dy in (0, 1, 3, 2)]
    ).astype(jnp.int32)
    place = lax.axis_index("x").astype(jnp.int32).reshape(1)
    positions, back, counts, order, filled, place = lax.optimization_barrier(
        (positions, back, counts, order, filled, place)
    )
    panels = PARTS[0][1] * KNB
    pieces = gather_pieces(take(incoming, positions[:panels]))
    gathered = lax.all_gather(take(incoming, positions[panels:]), ("y", "core"), axis=0)
    weights = (w_key, w_value, queries, out_grad)
    attended_0, grad_queries_0, shares, begun = attention(
        counts, order, pieces, *weights, PARTS[0], None
    )
    attended_1, grad_queries_1, shares, parts = attention(
        counts, order, gathered, *weights, PARTS[1], (begun, shares)
    )
    summed = lax.psum_scatter(shares, ("y", "core"), scatter_dimension=0)
    column = reduce_weight_grads(parts)
    returning = take(summed, back)
    returning, column = lax.optimization_barrier((returning, column))
    arrived = exchange(returning)
    grad_w_key, grad_w_value = spread_columns(column, place)
    grad_pool = collect(picked_slot, filled, arrived, pool.shape[0])
    return (
        jnp.concatenate([attended_0, attended_1]),
        jnp.concatenate([grad_queries_0, grad_queries_1]),
        grad_pool,
        grad_w_key,
        grad_w_value,
    )


def solution(mesh):
    grid = Mesh(mesh.devices.reshape(8, 4, 4, 2), ("z", "x", "y", "core"))
    seq, head = ("z", "x"), ("y", "core")
    return jax.shard_map(
        local,
        mesh=grid,
        in_specs=(
            P(seq, head),
            P(seq, head, None),
            P(None, head),
            P(None, head),
            P(seq, head),
            P(),
            P(),
            P(),
        ),
        out_specs=(
            P(seq, head),
            P(seq, head),
            P(seq, head, None),
            P(None, head),
            P(None, head),
        ),
        check_vma=False,
    )
```

```python
import functools
import math

import jax
import jax.numpy as jnp
from jax import lax
from jax.experimental import pallas as pl
from jax.experimental.pallas import tpu as pltpu
from jax.sharding import Mesh
from jax.sharding import PartitionSpec as P

DH = 128
STRETCH = 64
KNB = 2
CH_DEV = 16
ROWS = 16
PIECES = 8
SPAN = KNB * ROWS * PIECES
PARTS = ((0, 6, 3), (6, 10, 2))
F32 = jnp.float32
BF16 = jnp.bfloat16

UP = [(i, (i + 1) % 4) for i in range(4)]
DOWN = [((i + 1) % 4, i) for i in range(4)]
SWAP = [(0, 1), (1, 0)]


def dot(a, b, ca, cb):
    return lax.dot_general(a, b, (((ca,), (cb,)), ((), ())), preferred_element_type=F32)


def shift(size, k):
    return [(i, (i + k) % size) for i in range(size)]


def gather_pieces(own):
    half = own.shape[0] // 2
    below = lax.ppermute(own, "y", UP)
    above = lax.ppermute(own, "y", DOWN)
    far_low = lax.ppermute(below[:half], "y", UP)
    far_high = lax.ppermute(above[half:], "y", DOWN)
    mine = [own, above, below, far_low, far_high]
    return mine + [lax.ppermute(piece, "core", SWAP) for piece in mine]


def plus(*terms):
    total = terms[0].astype(F32)
    for term in terms[1:]:
        total = total + term.astype(F32)
    return total


def reduce_weight_grads(parts):
    by_x = lax.all_to_all(parts, "x", split_axis=0, concat_axis=0, tiled=True)
    part = plus(*[by_x[k] for k in range(4)]).astype(BF16).reshape(8, -1, DH)
    by_z = lax.all_to_all(part, "z", split_axis=0, concat_axis=0, tiled=True)
    total = plus(*[by_z[k] for k in range(8)]).astype(BF16)
    column = jnp.broadcast_to(total[None], part.shape)
    column = lax.all_to_all(column, "z", split_axis=0, concat_axis=0, tiled=True)
    return column.reshape(-1, DH)


def fill_from_pieces(step, group, half_steps, refs, rows_ref):
    for core in range(2):
        own, above, below, far_low, far_high = refs[core * 5 : core * 5 + 5]

        def put(place, ref):
            for c in range(group):
                at = c * SPAN + (core * 4 + place) * KNB * ROWS
                rows_ref[at : at + KNB * ROWS, :] = ref[c * KNB : (c + 1) * KNB].reshape(
                    KNB * ROWS, ref.shape[2]
                )

        put(0, own)
        put(1, above)
        put(2, below)

        @pl.when(step < half_steps)
        def _():
            put(3, far_low)

        @pl.when(step >= half_steps)
        def _():
            put(3, far_high)


def fill_from_gathered(group, gathered_ref, rows_ref):
    for piece in range(PIECES):
        for c in range(group):
            at = c * SPAN + piece * KNB * ROWS
            rows_ref[at : at + KNB * ROWS, :] = gathered_ref[
                piece, c * KNB : (c + 1) * KNB
            ].reshape(KNB * ROWS, gathered_ref.shape[3])


def attention_kernel(first, begin, stretch_count, group, count_ref, order_ref, *refs):
    step = pl.program_id(0)
    if first:
        pieces, refs = refs[:10], refs[10:]
    else:
        gathered_ref, begun_ref, _, refs = refs[0], refs[1], refs[2], refs[3:]
    key_weight_ref, value_weight_ref, query_ref, grad_ref, attended_ref, grad_query_ref = refs[:6]
    refs = refs[6:]
    share_ref, out_ref, rows_ref, kv_ref, both_ref, total_ref = refs
    if first:
        fill_from_pieces(step, group, stretch_count // group // 2, pieces, rows_ref)
    else:
        fill_from_gathered(group, gathered_ref, rows_ref)
    local = key_weight_ref.shape[1]
    factor = 1.0 / math.sqrt(DH)
    key_cols, value_cols = slice(0, local), slice(local, 2 * local)
    head_of = lax.broadcasted_iota(jnp.int32, (STRETCH, local), 1) < DH
    neighbour = (lax.broadcasted_iota(jnp.int32, (SPAN, 1), 0) // ROWS) % KNB

    def spread_heads(x):
        zero = jnp.zeros_like(x)
        return jnp.concatenate([jnp.where(head_of, x, zero), jnp.where(head_of, zero, x)], axis=0)

    def join_heads(x):
        return jnp.where(head_of, x[:STRETCH], x[STRETCH:])

    stretches = [
        (slice(c * SPAN, (c + 1) * SPAN), slice(c * STRETCH, (c + 1) * STRETCH))
        for c in range(group)
    ]
    for rows, _ in stretches:
        panel = rows_ref[rows, :]
        kv_ref[rows, key_cols] = dot(panel, key_weight_ref[...], 1, 0).astype(BF16)
        kv_ref[rows, value_cols] = dot(panel, value_weight_ref[...], 1, 0).astype(BF16)
    products = []
    for rows, tokens in stretches:
        query, grad = spread_heads(query_ref[tokens, :]), spread_heads(grad_ref[tokens, :])
        scores = dot(kv_ref[rows, key_cols], query, 1, 1) * factor
        dprobs = dot(kv_ref[rows, value_cols], grad, 1, 1)
        products.append((query, grad, scores, dprobs))
    softened = []
    for c in range(group):
        _, _, scores, dprobs = products[c]
        scores = jnp.where(neighbour < count_ref[begin + step * group + c], scores, -jnp.inf)
        powers = jnp.exp(scores - jnp.max(scores, axis=0, keepdims=True))
        probs = powers * (1.0 / jnp.sum(powers, axis=0, keepdims=True))
        row_dot = jnp.sum(probs * dprobs, axis=0, keepdims=True)
        softened.append((probs.astype(BF16), (probs * (dprobs - row_dot)).astype(BF16)))
    for c, (rows, tokens) in enumerate(stretches):
        query, grad, _, _ = products[c]
        weights, dscores = softened[c]
        both_ref[rows, key_cols] = (dot(dscores, query, 1, 0) * factor).astype(BF16)
        both_ref[rows, value_cols] = dot(weights, grad, 1, 0).astype(BF16)
        attended_ref[tokens, :] = join_heads(dot(weights, kv_ref[rows, value_cols], 0, 0)).astype(
            BF16
        )
        grad_query_ref[tokens, :] = (
            join_heads(dot(dscores, kv_ref[rows, key_cols], 0, 0)) * factor
        ).astype(BF16)
    for c, (rows, _) in enumerate(stretches):
        share = dot(both_ref[rows, key_cols], key_weight_ref[...], 1, 1)
        share = share + dot(both_ref[rows, value_cols], value_weight_ref[...], 1, 1)
        share = share.astype(BF16)
        for piece in range(PIECES):
            at = piece * KNB * ROWS
            part = share[at : at + KNB * ROWS].reshape(KNB, ROWS, share.shape[1])
            panels = slice(c * KNB, (c + 1) * KNB)
            share_ref[order_ref[piece] if first else piece, panels] = part
    part = dot(rows_ref[...], both_ref[...], 0, 0)

    @pl.when(step == 0)
    def _():
        total_ref[...] = part if first else begun_ref[...].astype(F32) + part

    @pl.when(step > 0)
    def _():
        total_ref[...] += part

    @pl.when(step == pl.num_programs(0) - 1)
    def _():
        if first:
            out_ref[...] = total_ref[...].astype(BF16)
        else:
            for g in range(4):
                out_ref[g] = total_ref[:, g * DH : (g + 1) * DH].astype(BF16)


def attention(counts, order, panels, w_key, w_value, queries, out_grad, part, begun):
    width, local = w_key.shape
    begin, stretch_count, group = part
    tokens = stretch_count * STRETCH
    steps, skip = stretch_count // group, begin // group
    half_steps = steps // 2
    first = begun is None
    block = (group * KNB, ROWS, width)
    plain = pl.BlockSpec(block, lambda i, *_: (i, 0, 0))
    low = pl.BlockSpec(block, lambda i, *_: (jnp.minimum(i, half_steps - 1), 0, 0))
    high = pl.BlockSpec(block, lambda i, *_: (jnp.maximum(i - half_steps, 0), 0, 0))
    stacked = lambda skip: pl.BlockSpec((PIECES,) + block, lambda i, *_: (0, skip + i, 0, 0))
    shares = jax.ShapeDtypeStruct((PIECES, CH_DEV * KNB, ROWS, width), BF16)
    token_in = pl.BlockSpec((group * STRETCH, local), lambda i, *_: (i + skip, 0))
    token_out = pl.BlockSpec((group * STRETCH, local), lambda i, *_: (i, 0))
    token_shape = jax.ShapeDtypeStruct((tokens, local), BF16)
    whole = lambda shape: pl.BlockSpec(shape, lambda i, *_: (0,) * len(shape))
    total = (width, 2 * local)
    scratch = [
        pltpu.VMEM((group * SPAN, width), BF16),
        pltpu.VMEM((group * SPAN, 2 * local), BF16),
        pltpu.VMEM((group * SPAN, 2 * local), BF16),
        pltpu.VMEM(total, F32),
    ]
    if first:
        in_specs = [plain, plain, plain, low, high] * 2
        out = jax.ShapeDtypeStruct(total, BF16)
        aliases = {}
    else:
        in_specs = [stacked(0), whole(total), pl.BlockSpec(memory_space=pl.ANY)]
        panels = (panels,) + begun
        out = jax.ShapeDtypeStruct((4, width, DH), BF16)
        aliases = {4: 2}
    return pl.pallas_call(
        functools.partial(attention_kernel, first, begin, stretch_count, group),
        grid_spec=pltpu.PrefetchScalarGridSpec(
            num_scalar_prefetch=2,
            grid=(steps,),
            in_specs=in_specs + [whole(w_key.shape), whole(w_key.shape), token_in, token_in],
            out_specs=[token_out, token_out, stacked(skip), whole(out.shape)],
            scratch_shapes=scratch,
        ),
        out_shape=[token_shape, token_shape, shares, out],
        input_output_aliases=aliases,
        compiler_params=pltpu.CompilerParams(vmem_limit_bytes=51 * 2**20),
        cost_estimate=pl.CostEstimate(
            flops=8 * 2**30, bytes_accessed=16 * 2**20, transcendentals=2**18
        ),
        name="attention",
    )(counts, order, *panels, w_key, w_value, queries, out_grad)


def collect_kernel(slot_ref, filled_ref, arrived_ref, out_ref):
    out_ref[...] = jnp.zeros_like(out_ref)

    def one(q, carry):
        @pl.when(filled_ref[q] != 0)
        def _():
            out_ref[slot_ref[q]] += arrived_ref[q].astype(F32)

        return carry

    lax.fori_loop(0, slot_ref.shape[0], one, 0)


def collect(slots, filled, arrived, pool_count):
    count, rows, width = arrived.shape
    return pl.pallas_call(
        collect_kernel,
        grid_spec=pltpu.PrefetchScalarGridSpec(
            num_scalar_prefetch=2,
            grid=(1,),
            in_specs=[pl.BlockSpec((count, rows, width), lambda i, *_: (0, 0, 0))],
            out_specs=pl.BlockSpec((pool_count, rows, width), lambda i, *_: (0, 0, 0)),
        ),
        out_shape=jax.ShapeDtypeStruct((pool_count, rows, width), F32),
        compiler_params=pltpu.CompilerParams(vmem_limit_bytes=16 * 2**20),
        name="collect",
    )(slots, filled, arrived)


def spread_kernel(place_ref, *refs):
    pieces, (key_ref, value_ref, held_ref) = refs[:4], refs[4:]
    for k in range(4):
        held_ref[lax.rem(place_ref[0] - k + 4, 4)] = pieces[k][...].astype(F32)
    key_ref[:, :DH], key_ref[:, DH:] = held_ref[0], held_ref[1]
    value_ref[:, :DH], value_ref[:, DH:] = held_ref[2], held_ref[3]


def spread_columns(column, place):
    width = column.shape[0]
    pieces = [column] + [lax.ppermute(column, "x", shift(4, k)) for k in (1, 3, 2)]
    pieces = [pieces[0], pieces[1], pieces[3], pieces[2]]
    shape = jax.ShapeDtypeStruct((width, 2 * DH), F32)
    return pl.pallas_call(
        spread_kernel,
        grid_spec=pltpu.PrefetchScalarGridSpec(
            num_scalar_prefetch=1,
            grid=(1,),
            in_specs=[pl.BlockSpec(column.shape, lambda i, *_: (0, 0))] * 4,
            out_specs=[pl.BlockSpec(shape.shape, lambda i, *_: (0, 0))] * 2,
            scratch_shapes=[pltpu.VMEM((4, width, DH), F32)],
        ),
        out_shape=[shape, shape],
        compiler_params=pltpu.CompilerParams(vmem_limit_bytes=16 * 2**20),
        name="spread",
    )(place, *pieces)


def exchange(array):
    return lax.all_to_all(array, ("z", "x"), split_axis=0, concat_axis=0, tiled=True)


def local(queries, pool, w_key, w_value, out_grad, nb_source, nb_slot, nb_count):
    seq_count = lax.axis_size(("z", "x"))
    seq_index = lax.axis_index(("z", "x"))
    requests = CH_DEV * KNB
    capacity = max(2, 2 * requests // seq_count)
    slot_span = seq_count * capacity
    pool_count = pool.shape[0]
    packed = (nb_source * pool_count + nb_slot).reshape(seq_count, requests)
    source_table, slot_table = packed // pool_count, packed % pool_count
    order_ids = jnp.arange(requests)
    matches = source_table[:, :, None] == source_table[:, None, :]
    before = order_ids[None, :] < order_ids[:, None]
    ranks = jnp.sum(jnp.logical_and(matches, before[None, :, :]), axis=2)
    places = jnp.arange(capacity)
    chosen = jnp.logical_and(
        (source_table == seq_index)[:, :, None], ranks[:, :, None] == places[None, None, :]
    )
    picked_slot = jnp.sum(jnp.where(chosen, slot_table[:, :, None], 0), axis=1).reshape(slot_span)
    filled = jnp.any(chosen, axis=1).reshape(slot_span).astype(jnp.int32)
    own_sources = lax.dynamic_index_in_dim(source_table, seq_index, 0, keepdims=False)
    own_ranks = lax.dynamic_index_in_dim(ranks, seq_index, 0, keepdims=False)
    positions = own_sources * capacity + own_ranks
    back = jnp.sum(
        jnp.where(positions[None, :] == jnp.arange(slot_span)[:, None], order_ids[None, :], 0), axis=1
    )
    counts = lax.dynamic_slice_in_dim(nb_count, seq_index * CH_DEV, CH_DEV)
    take = lambda array, index: jnp.take(array, index, axis=0, mode="clip")

    incoming = exchange(take(pool, picked_slot))
    y, core = lax.axis_index("y"), lax.axis_index("core")
    order = jnp.stack(
        [(y + dy) % 4 * 2 + (core + other) % 2 for other in (0, 1) for dy in (0, 1, 3, 2)]
    ).astype(jnp.int32)
    place = lax.axis_index("x").astype(jnp.int32).reshape(1)
    positions, back, counts, order, filled, place = lax.optimization_barrier(
        (positions, back, counts, order, filled, place)
    )
    panels = PARTS[0][1] * KNB
    pieces = gather_pieces(take(incoming, positions[:panels]))
    gathered = lax.all_gather(take(incoming, positions[panels:]), ("y", "core"), axis=0)
    weights = (w_key, w_value, queries, out_grad)
    attended_0, grad_queries_0, shares, begun = attention(
        counts, order, pieces, *weights, PARTS[0], None
    )
    attended_1, grad_queries_1, shares, parts = attention(
        counts, order, gathered, *weights, PARTS[1], (begun, shares)
    )
    summed = lax.psum_scatter(shares, ("y", "core"), scatter_dimension=0)
    column = reduce_weight_grads(parts)
    returning = take(summed, back)
    returning, column = lax.optimization_barrier((returning, column))
    arrived = exchange(returning)
    grad_w_key, grad_w_value = spread_columns(column, place)
    grad_pool = collect(picked_slot, filled, arrived, pool.shape[0])
    return (
        jnp.concatenate([attended_0, attended_1]),
        jnp.concatenate([grad_queries_0, grad_queries_1]),
        grad_pool,
        grad_w_key,
        grad_w_value,
    )


def solution(mesh):
    grid = Mesh(mesh.devices.reshape(8, 4, 4, 2), ("z", "x", "y", "core"))
    seq, head = ("z", "x"), ("y", "core")
    return jax.shard_map(
        local,
        mesh=grid,
        in_specs=(
            P(seq, head),
            P(seq, head, None),
            P(None, head),
            P(None, head),
            P(seq, head),
            P(),
            P(),
            P(),
        ),
        out_specs=(
            P(seq, head),
            P(seq, head),
            P(seq, head, None),
            P(None, head),
            P(None, head),
        ),
        check_vma=False,
    )
```

```python
import functools
import math

import jax
import jax.numpy as jnp
from jax import lax
from jax.experimental import pallas as pl
from jax.experimental.pallas import tpu as pltpu
from jax.sharding import Mesh
from jax.sharding import PartitionSpec as P

DH = 128
STRETCH = 64
KNB = 2
CH_DEV = 16
ROWS = 16
PIECES = 8
SPAN = KNB * ROWS * PIECES
PARTS = ((0, 6, 3), (6, 10, 2))
F32 = jnp.float32
BF16 = jnp.bfloat16

UP = [(i, (i + 1) % 4) for i in range(4)]
DOWN = [((i + 1) % 4, i) for i in range(4)]
SWAP = [(0, 1), (1, 0)]


def dot(a, b, ca, cb):
    return lax.dot_general(a, b, (((ca,), (cb,)), ((), ())), preferred_element_type=F32)


def shift(size, k):
    return [(i, (i + k) % size) for i in range(size)]


def gather_pieces(own):
    half = own.shape[0] // 2
    below = lax.ppermute(own, "y", UP)
    above = lax.ppermute(own, "y", DOWN)
    far_low = lax.ppermute(below[:half], "y", UP)
    far_high = lax.ppermute(above[half:], "y", DOWN)
    mine = [own, above, below, far_low, far_high]
    return mine + [lax.ppermute(piece, "core", SWAP) for piece in mine]


def plus(*terms):
    total = terms[0].astype(F32)
    for term in terms[1:]:
        total = total + term.astype(F32)
    return total


def reduce_weight_grads(parts):
    by_x = lax.all_to_all(parts, "x", split_axis=0, concat_axis=0, tiled=True)
    part = plus(*[by_x[k] for k in range(4)]).astype(BF16).reshape(8, -1, DH)
    by_z = lax.all_to_all(part, "z", split_axis=0, concat_axis=0, tiled=True)
    total = plus(*[by_z[k] for k in range(8)]).astype(BF16)
    column = jnp.broadcast_to(total[None], part.shape)
    column = lax.all_to_all(column, "z", split_axis=0, concat_axis=0, tiled=True)
    return column.reshape(-1, DH)


def fill_from_pieces(step, group, half_steps, refs, rows_ref):
    for core in range(2):
        own, above, below, far_low, far_high = refs[core * 5 : core * 5 + 5]

        def put(place, ref):
            for c in range(group):
                at = c * SPAN + (core * 4 + place) * KNB * ROWS
                rows_ref[at : at + KNB * ROWS, :] = ref[c * KNB : (c + 1) * KNB].reshape(
                    KNB * ROWS, ref.shape[2]
                )

        put(0, own)
        put(1, above)
        put(2, below)

        @pl.when(step < half_steps)
        def _():
            put(3, far_low)

        @pl.when(step >= half_steps)
        def _():
            put(3, far_high)


def fill_from_gathered(group, gathered_ref, rows_ref):
    for piece in range(PIECES):
        for c in range(group):
            at = c * SPAN + piece * KNB * ROWS
            rows_ref[at : at + KNB * ROWS, :] = gathered_ref[
                piece, c * KNB : (c + 1) * KNB
            ].reshape(KNB * ROWS, gathered_ref.shape[3])


def attention_kernel(first, begin, stretch_count, group, count_ref, order_ref, *refs):
    step = pl.program_id(0)
    if first:
        pieces, refs = refs[:10], refs[10:]
    else:
        gathered_ref, begun_ref, _, refs = refs[0], refs[1], refs[2], refs[3:]
    key_weight_ref, value_weight_ref, query_ref, grad_ref, attended_ref, grad_query_ref = refs[:6]
    refs = refs[6:]
    share_ref, out_ref, rows_ref, kv_ref, both_ref, total_ref = refs
    if first:
        fill_from_pieces(step, group, stretch_count // group // 2, pieces, rows_ref)
    else:
        fill_from_gathered(group, gathered_ref, rows_ref)
    local = key_weight_ref.shape[1]
    factor = 1.0 / math.sqrt(DH)
    key_cols, value_cols = slice(0, local), slice(local, 2 * local)
    head_of = lax.broadcasted_iota(jnp.int32, (STRETCH, local), 1) < DH
    neighbour = (lax.broadcasted_iota(jnp.int32, (SPAN, 1), 0) // ROWS) % KNB

    def spread_heads(x):
        zero = jnp.zeros_like(x)
        return jnp.concatenate([jnp.where(head_of, x, zero), jnp.where(head_of, zero, x)], axis=0)

    def join_heads(x):
        return jnp.where(head_of, x[:STRETCH], x[STRETCH:])

    stretches = [
        (slice(c * SPAN, (c + 1) * SPAN), slice(c * STRETCH, (c + 1) * STRETCH))
        for c in range(group)
    ]
    for rows, _ in stretches:
        panel = rows_ref[rows, :]
        kv_ref[rows, key_cols] = dot(panel, key_weight_ref[...], 1, 0).astype(BF16)
        kv_ref[rows, value_cols] = dot(panel, value_weight_ref[...], 1, 0).astype(BF16)
    products = []
    for rows, tokens in stretches:
        query, grad = spread_heads(query_ref[tokens, :]), spread_heads(grad_ref[tokens, :])
        scores = dot(kv_ref[rows, key_cols], query, 1, 1) * factor
        dprobs = dot(kv_ref[rows, value_cols], grad, 1, 1)
        products.append((query, grad, scores, dprobs))
    softened = []
    for c in range(group):
        _, _, scores, dprobs = products[c]
        scores = jnp.where(neighbour < count_ref[begin + step * group + c], scores, -jnp.inf)
        powers = jnp.exp(scores - jnp.max(scores, axis=0, keepdims=True))
        probs = powers * (1.0 / jnp.sum(powers, axis=0, keepdims=True))
        row_dot = jnp.sum(probs * dprobs, axis=0, keepdims=True)
        softened.append((probs.astype(BF16), (probs * (dprobs - row_dot)).astype(BF16)))
    for c, (rows, tokens) in enumerate(stretches):
        query, grad, _, _ = products[c]
        weights, dscores = softened[c]
        both_ref[rows, key_cols] = (dot(dscores, query, 1, 0) * factor).astype(BF16)
        both_ref[rows, value_cols] = dot(weights, grad, 1, 0).astype(BF16)
        attended_ref[tokens, :] = join_heads(dot(weights, kv_ref[rows, value_cols], 0, 0)).astype(
            BF16
        )
        grad_query_ref[tokens, :] = (
            join_heads(dot(dscores, kv_ref[rows, key_cols], 0, 0)) * factor
        ).astype(BF16)
    for c, (rows, _) in enumerate(stretches):
        share = dot(both_ref[rows, key_cols], key_weight_ref[...], 1, 1)
        share = share + dot(both_ref[rows, value_cols], value_weight_ref[...], 1, 1)
        share = share.astype(BF16)
        for piece in range(PIECES):
            at = piece * KNB * ROWS
            part = share[at : at + KNB * ROWS].reshape(KNB, ROWS, share.shape[1])
            panels = slice(c * KNB, (c + 1) * KNB)
            share_ref[order_ref[piece] if first else piece, panels] = part
    part = dot(rows_ref[...], both_ref[...], 0, 0)

    @pl.when(step == 0)
    def _():
        total_ref[...] = part if first else begun_ref[...].astype(F32) + part

    @pl.when(step > 0)
    def _():
        total_ref[...] += part

    @pl.when(step == pl.num_programs(0) - 1)
    def _():
        if first:
            out_ref[...] = total_ref[...].astype(BF16)
        else:
            for g in range(4):
                out_ref[g] = total_ref[:, g * DH : (g + 1) * DH].astype(BF16)


def attention(counts, order, panels, w_key, w_value, queries, out_grad, part, begun):
    width, local = w_key.shape
    begin, stretch_count, group = part
    tokens = stretch_count * STRETCH
    steps, skip = stretch_count // group, begin // group
    half_steps = steps // 2
    first = begun is None
    block = (group * KNB, ROWS, width)
    plain = pl.BlockSpec(block, lambda i, *_: (i, 0, 0))
    low = pl.BlockSpec(block, lambda i, *_: (jnp.minimum(i, half_steps - 1), 0, 0))
    high = pl.BlockSpec(block, lambda i, *_: (jnp.maximum(i - half_steps, 0), 0, 0))
    stacked = lambda skip: pl.BlockSpec((PIECES,) + block, lambda i, *_: (0, skip + i, 0, 0))
    shares = jax.ShapeDtypeStruct((PIECES, CH_DEV * KNB, ROWS, width), BF16)
    token_in = pl.BlockSpec((group * STRETCH, local), lambda i, *_: (i + skip, 0))
    token_out = pl.BlockSpec((group * STRETCH, local), lambda i, *_: (i, 0))
    token_shape = jax.ShapeDtypeStruct((tokens, local), BF16)
    whole = lambda shape: pl.BlockSpec(shape, lambda i, *_: (0,) * len(shape))
    total = (width, 2 * local)
    scratch = [
        pltpu.VMEM((group * SPAN, width), BF16),
        pltpu.VMEM((group * SPAN, 2 * local), BF16),
        pltpu.VMEM((group * SPAN, 2 * local), BF16),
        pltpu.VMEM(total, F32),
    ]
    if first:
        in_specs = [plain, plain, plain, low, high] * 2
        out = jax.ShapeDtypeStruct(total, BF16)
        aliases = {}
    else:
        in_specs = [stacked(0), whole(total), pl.BlockSpec(memory_space=pl.ANY)]
        panels = (panels,) + begun
        out = jax.ShapeDtypeStruct((4, width, DH), BF16)
        aliases = {4: 2}
    return pl.pallas_call(
        functools.partial(attention_kernel, first, begin, stretch_count, group),
        grid_spec=pltpu.PrefetchScalarGridSpec(
            num_scalar_prefetch=2,
            grid=(steps,),
            in_specs=in_specs + [whole(w_key.shape), whole(w_key.shape), token_in, token_in],
            out_specs=[token_out, token_out, stacked(skip), whole(out.shape)],
            scratch_shapes=scratch,
        ),
        out_shape=[token_shape, token_shape, shares, out],
        input_output_aliases=aliases,
        compiler_params=pltpu.CompilerParams(vmem_limit_bytes=56 * 2**20),
        cost_estimate=pl.CostEstimate(
            flops=8 * 2**30, bytes_accessed=16 * 2**20, transcendentals=2**18
        ),
        name="attention",
    )(counts, order, *panels, w_key, w_value, queries, out_grad)


def collect_kernel(slot_ref, filled_ref, arrived_ref, out_ref):
    out_ref[...] = jnp.zeros_like(out_ref)

    def one(q, carry):
        @pl.when(filled_ref[q] != 0)
        def _():
            out_ref[slot_ref[q]] += arrived_ref[q].astype(F32)

        return carry

    lax.fori_loop(0, slot_ref.shape[0], one, 0)


def collect(slots, filled, arrived, pool_count):
    count, rows, width = arrived.shape
    return pl.pallas_call(
        collect_kernel,
        grid_spec=pltpu.PrefetchScalarGridSpec(
            num_scalar_prefetch=2,
            grid=(1,),
            in_specs=[pl.BlockSpec((count, rows, width), lambda i, *_: (0, 0, 0))],
            out_specs=pl.BlockSpec((pool_count, rows, width), lambda i, *_: (0, 0, 0)),
        ),
        out_shape=jax.ShapeDtypeStruct((pool_count, rows, width), F32),
        compiler_params=pltpu.CompilerParams(vmem_limit_bytes=16 * 2**20),
        name="collect",
    )(slots, filled, arrived)


def spread_kernel(place_ref, *refs):
    pieces, (key_ref, value_ref, held_ref) = refs[:4], refs[4:]
    for k in range(4):
        held_ref[lax.rem(place_ref[0] - k + 4, 4)] = pieces[k][...].astype(F32)
    key_ref[:, :DH], key_ref[:, DH:] = held_ref[0], held_ref[1]
    value_ref[:, :DH], value_ref[:, DH:] = held_ref[2], held_ref[3]


def spread_columns(column, place):
    width = column.shape[0]
    pieces = [column] + [lax.ppermute(column, "x", shift(4, k)) for k in (2, 3, 1)]
    pieces = [pieces[0], pieces[3], pieces[1], pieces[2]]
    shape = jax.ShapeDtypeStruct((width, 2 * DH), F32)
    return pl.pallas_call(
        spread_kernel,
        grid_spec=pltpu.PrefetchScalarGridSpec(
            num_scalar_prefetch=1,
            grid=(1,),
            in_specs=[pl.BlockSpec(column.shape, lambda i, *_: (0, 0))] * 4,
            out_specs=[pl.BlockSpec(shape.shape, lambda i, *_: (0, 0))] * 2,
            scratch_shapes=[pltpu.VMEM((4, width, DH), F32)],
        ),
        out_shape=[shape, shape],
        compiler_params=pltpu.CompilerParams(vmem_limit_bytes=16 * 2**20),
        name="spread",
    )(place, *pieces)


def exchange(array):
    return lax.all_to_all(array, ("z", "x"), split_axis=0, concat_axis=0, tiled=True)


def local(queries, pool, w_key, w_value, out_grad, nb_source, nb_slot, nb_count):
    seq_count = lax.axis_size(("z", "x"))
    seq_index = lax.axis_index(("z", "x"))
    requests = CH_DEV * KNB
    capacity = max(2, 2 * requests // seq_count)
    slot_span = seq_count * capacity
    pool_count = pool.shape[0]
    packed = (nb_source * pool_count + nb_slot).reshape(seq_count, requests)
    source_table, slot_table = packed // pool_count, packed % pool_count
    order_ids = jnp.arange(requests)
    matches = source_table[:, :, None] == source_table[:, None, :]
    before = order_ids[None, :] < order_ids[:, None]
    ranks = jnp.sum(jnp.logical_and(matches, before[None, :, :]), axis=2)
    places = jnp.arange(capacity)
    chosen = jnp.logical_and(
        (source_table == seq_index)[:, :, None], ranks[:, :, None] == places[None, None, :]
    )
    picked_slot = jnp.sum(jnp.where(chosen, slot_table[:, :, None], 0), axis=1).reshape(slot_span)
    filled = jnp.any(chosen, axis=1).reshape(slot_span).astype(jnp.int32)
    own_sources = lax.dynamic_index_in_dim(source_table, seq_index, 0, keepdims=False)
    own_ranks = lax.dynamic_index_in_dim(ranks, seq_index, 0, keepdims=False)
    positions = own_sources * capacity + own_ranks
    back = jnp.sum(
        jnp.where(positions[None, :] == jnp.arange(slot_span)[:, None], order_ids[None, :], 0), axis=1
    )
    counts = lax.dynamic_slice_in_dim(nb_count, seq_index * CH_DEV, CH_DEV)
    take = lambda array, index: jnp.take(array, index, axis=0, mode="clip")

    incoming = exchange(take(pool, picked_slot))
    y, core = lax.axis_index("y"), lax.axis_index("core")
    order = jnp.stack(
        [(y + dy) % 4 * 2 + (core + other) % 2 for other in (0, 1) for dy in (0, 1, 3, 2)]
    ).astype(jnp.int32)
    place = lax.axis_index("x").astype(jnp.int32).reshape(1)
    positions, back, counts, order, filled, place = lax.optimization_barrier(
        (positions, back, counts, order, filled, place)
    )
    panels = PARTS[0][1] * KNB
    wanted, later = lax.optimization_barrier(
        (take(incoming, positions[:panels]), take(incoming, positions[panels:]))
    )
    pieces = gather_pieces(wanted)
    gathered = lax.all_gather(later, ("y", "core"), axis=0)
    weights = (w_key, w_value, queries, out_grad)
    attended_0, grad_queries_0, shares, begun = attention(
        counts, order, pieces, *weights, PARTS[0], None
    )
    attended_1, grad_queries_1, shares, parts = attention(
        counts, order, gathered, *weights, PARTS[1], (begun, shares)
    )
    summed = lax.psum_scatter(shares, ("y", "core"), scatter_dimension=0)
    column = reduce_weight_grads(parts)
    returning = take(summed, back)
    returning, column = lax.optimization_barrier((returning, column))
    arrived = exchange(returning)
    grad_w_key, grad_w_value = spread_columns(column, place)
    grad_pool = collect(picked_slot, filled, arrived, pool.shape[0])
    return (
        jnp.concatenate([attended_0, attended_1]),
        jnp.concatenate([grad_queries_0, grad_queries_1]),
        grad_pool,
        grad_w_key,
        grad_w_value,
    )


def solution(mesh):
    grid = Mesh(mesh.devices.reshape(8, 4, 4, 2), ("z", "x", "y", "core"))
    seq, head = ("z", "x"), ("y", "core")
    return jax.shard_map(
        local,
        mesh=grid,
        in_specs=(
            P(seq, head),
            P(seq, head, None),
            P(None, head),
            P(None, head),
            P(seq, head),
            P(),
            P(),
            P(),
        ),
        out_specs=(
            P(seq, head),
            P(seq, head),
            P(seq, head, None),
            P(None, head),
            P(None, head),
        ),
        check_vma=False,
    )
```
